128 devices in a mesh: dp: 16 (over x, y_lo, core), seq: 8 (over y_hi, z).
Axes of the slice: x: 4, y: 4 (y_hi: 2, y_lo: 2; y = y_hi * 2 + y_lo), z: 4, core: 2. Of those that a mesh axis runs over, the one named last changes fastest.
Arguments:
- queries: bfloat16 [16, 512, 5120], P('dp', 'seq'), may hold values from -64 to 64
- keys: bfloat16 [16, 2048, 5120], P('dp', 'seq'), may hold values from -6 to 6
- values: bfloat16 [16, 2048, 5120], P('dp', 'seq'), may hold values from -6 to 6
- out_grad: bfloat16 [16, 512, 5120], P('dp', 'seq'), may hold values from -192 to 192
- layer_input: bfloat16 [16, 2048, 5120], P('dp', 'seq'), may hold values from -6 to 6
- projection: bfloat16 [5120, 512], replicated, may hold values from -0.078125 to 0.078125
- token_counts: int32 [16], P('dp'), may hold values from 1024 to 2048, as said below
- slab_start: int32 [16], P('dp'), may hold values from 0 to 1536
Outputs:
- query_grad: bfloat16 [16, 512, 5120], P('dp', 'seq')
- projected_grads: float32 [512, 2, 5120], P(('dp', 'seq'))
The draws below stay inside these ranges and needn't reach their ends.
Inputs may be any that keep to these rules, and one draw needn't show every extreme that they name: `token_counts`: some clip has 2048 valid tokens and some clip 2048 // 2.
All inputs are finite; a program needn't handle non-finite values.
Results may differ from the reference program's by a relative error of at most 0.0057.
Values may be sent and summed in bfloat16 or wider, within the bound.
No kernel may reach another device: no remote copies, remote signals or barrier semaphores. Data moves between devices by JAX's collectives and lax.ppermute only.
A program may use at most 192 MiB of HBM per device.

```python
import jax
import jax.numpy as jnp
from jax import lax

D = 5120
HEADS = 40
HEAD_DIM = 128
RANK = 512
CLIPS = 16
SLAB = 512
KEYS = 2048


def pair_fields(key):
    query_key = jax.random.fold_in(key, 11)
    keys_key = jax.random.fold_in(key, 12)
    query_vals = jax.random.truncated_normal(query_key, -6.0, 6.0, (CLIPS, SLAB, D), jnp.float32)
    keys_vals = jax.random.truncated_normal(keys_key, -6.0, 6.0, (CLIPS, KEYS, D), jnp.float32)
    return (query_vals, keys_vals)


def draw_queries(key, part):
    return pair_fields(key)[0].astype(jnp.bfloat16)


def draw_keys(key, part):
    return pair_fields(key)[1].astype(jnp.bfloat16)


def draw_token_counts(key, part):
    counts = jax.random.randint(jax.random.fold_in(key, 21), (CLIPS,), KEYS // 2, KEYS + 1, jnp.int32)
    counts = counts.at[0].set(KEYS)
    return counts.at[CLIPS - 1].set(KEYS // 2)


def draw_slab_start(key, part):
    starts = jax.random.randint(jax.random.fold_in(key, 22), (CLIPS,), 0, KEYS - SLAB + 1, jnp.int32)
    starts = starts.at[0].set(0)
    return starts.at[1].set(KEYS - SLAB)


def level_of(key, shape, cuts, low, high):
    gain, own = 1.0, jax.random.fold_in(key, 6)
    for axis_at, blocks in cuts:
        heights = jnp.exp(jax.random.uniform(jax.random.fold_in(own, axis_at), (blocks,), jnp.float32, low / len(cuts), high / len(cuts)))
        gain = gain * jnp.repeat(heights, shape[axis_at] // blocks).reshape([-1 if axis == axis_at else 1 for axis in range(len(shape))])
    return gain


def gaussian(own_key, shape, deviation, bound, cuts=(), kind=jnp.bfloat16):
    values = jax.random.normal(own_key, shape, jnp.float32) * deviation
    if len(cuts) > 0:
        values = level_of(own_key, shape, cuts, -0.22, 0.18) * values
    return jnp.clip(values, min=-bound, max=bound).astype(kind)


def setup_inputs(seed: int = 0) -> dict:
    arg_keys = jax.random.split(jax.random.key(seed), 9)
    queries = draw_queries(jax.random.fold_in(arg_keys[8], 71), 0)
    keys = draw_keys(jax.random.fold_in(arg_keys[8], 71), 0)
    values = gaussian(arg_keys[2], (CLIPS, KEYS, D), 1.0, 6.0, ((0, 16), (1, 8)))
    out_grad = gaussian(arg_keys[3], (CLIPS, SLAB, D), 32.0, 192.0, ((0, 16), (1, 8)))
    layer_input = gaussian(arg_keys[4], (CLIPS, KEYS, D), 1.0, 6.0, ((0, 16), (1, 8)))
    projection = gaussian(arg_keys[5], (D, RANK), D ** -0.5, 0.078125)
    token_counts = draw_token_counts(jax.random.fold_in(arg_keys[8], 71), 0)
    slab_start = draw_slab_start(jax.random.fold_in(arg_keys[8], 71), 0)
    return {"queries": queries, "keys": keys, "values": values, "out_grad": out_grad, "layer_input": layer_input, "projection": projection, "token_counts": token_counts, "slab_start": slab_start}


def head_grads(query_block, key_block, value_block, grad_block, key_valid):
    scale_qk = HEAD_DIM ** -0.5
    scores = jnp.dot(query_block, key_block.T, preferred_element_type=jnp.float32) * scale_qk
    scores = jnp.where(key_valid[None, :], scores, -1e30)
    row_max = jnp.max(scores, axis=1, keepdims=True)
    expo = jnp.exp(scores - row_max)
    weights = expo / jnp.sum(expo, axis=1, keepdims=True)
    weight_half = weights.astype(jnp.bfloat16)
    grad_probs = jnp.dot(grad_block, value_block.T, preferred_element_type=jnp.float32)
    row_dot = jnp.sum(weights * grad_probs, axis=1, keepdims=True)
    grad_scores = (weights * (grad_probs - row_dot)).astype(jnp.bfloat16)
    query_grad = (jnp.dot(grad_scores, key_block, preferred_element_type=jnp.float32) * scale_qk).astype(jnp.bfloat16)
    key_grad = (jnp.dot(grad_scores.T, query_block, preferred_element_type=jnp.float32) * scale_qk).astype(jnp.bfloat16)
    value_grad = jnp.dot(weight_half.T, grad_block, preferred_element_type=jnp.float32).astype(jnp.bfloat16)
    return query_grad, key_grad, value_grad


def to_heads(array):
    return jnp.moveaxis(array.reshape(array.shape[0], HEADS, HEAD_DIM), 1, 0)


def to_rows(array):
    return jnp.moveaxis(array, 0, 1).reshape(array.shape[1], HEADS * HEAD_DIM)


def clip_pass(items):
    query_c, keys_c, values_c, grad_c, input_c, projection, count_c, start_c = items
    query_valid = (start_c + jnp.arange(SLAB, dtype=jnp.int32)) < count_c
    key_valid = jnp.arange(KEYS, dtype=jnp.int32) < count_c
    masked_grad = jnp.where(query_valid[:, None], grad_c, jnp.zeros_like(grad_c))

    def one_head(parts):
        return head_grads(parts[0], parts[1], parts[2], parts[3], key_valid)

    dq_heads, dk_heads, dv_heads = lax.map(one_head, (to_heads(query_c), to_heads(keys_c), to_heads(values_c), to_heads(masked_grad)))
    key_grad = to_rows(dk_heads)
    value_grad = to_rows(dv_heads)
    input_low = jnp.dot(input_c, projection, preferred_element_type=jnp.float32).astype(jnp.bfloat16)
    grad_k = jnp.einsum("tr,td->rd", input_low, key_grad, preferred_element_type=jnp.float32)
    grad_v = jnp.einsum("tr,td->rd", input_low, value_grad, preferred_element_type=jnp.float32)
    return to_rows(dq_heads), jnp.stack([grad_k, grad_v], axis=1)


def reference(queries, keys, values, out_grad, layer_input, projection, token_counts, slab_start):
    def step(total, items):
        dq_clip, grads_clip = clip_pass((items[0], items[1], items[2], items[3], items[4], projection, items[5], items[6]))
        return total + grads_clip, dq_clip

    start_total = jnp.zeros((RANK, 2, HEADS * HEAD_DIM), jnp.float32)
    total, query_grad = lax.scan(step, start_total, (queries, keys, values, out_grad, layer_input, token_counts, slab_start))
    return query_grad, total * (1.0 / CLIPS)
```

```python
import functools
import math

import jax
import jax.numpy as jnp
from jax import lax
from jax.experimental import pallas as pl
from jax.experimental.pallas import tpu as pltpu
from jax.sharding import PartitionSpec as P

HEAD_DIM = 128
VMEM_LIMIT = 40 * 1024 * 1024


def pack_kernel(pieces, k_ref, v_ref, q_ref, g_ref, *outs):
    for heads, out in zip(pieces, outs):
        row = 0
        for head in heads:
            for src in (k_ref, v_ref, q_ref, g_ref):
                rows = src.shape[0]
                out[0, row : row + rows, :] = src[:, head * HEAD_DIM : (head + 1) * HEAD_DIM]
                row += rows


def pack(keys, values, queries, grads, pieces, groups):
    kt, width = keys.shape
    qt = queries.shape[0]
    rows = 2 * kt + 2 * qt
    return pl.pallas_call(
        functools.partial(pack_kernel, pieces),
        grid=(groups,),
        out_shape=[jax.ShapeDtypeStruct((groups, len(p) * rows, HEAD_DIM), keys.dtype) for p in pieces],
        in_specs=[pl.BlockSpec((n, width // groups), lambda j: (0, j)) for n in (kt, kt, qt, qt)],
        out_specs=[pl.BlockSpec((1, len(p) * rows, HEAD_DIM), lambda j: (j, 0, 0)) for p in pieces],
        cost_estimate=pl.CostEstimate(flops=0, transcendentals=0, bytes_accessed=4 * rows * width),
    )(keys, values, queries, grads)


def unpack_kernel(groups, spots, nparts, source_ref, *refs):
    ins, out_ref = refs[:-1], refs[-1]
    per_group = sum(spots)
    rows = out_ref.shape[0]
    for k in range(groups):
        j = source_ref[k]
        head = 0
        for n in range(nparts):
            for m in range(spots[n]):
                column = pl.multiple_of((j * per_group + head) * HEAD_DIM, HEAD_DIM)
                out_ref[:, pl.ds(column, HEAD_DIM)] = ins[n * groups + k][m * rows : (m + 1) * rows, :]
                head += 1


def unpack(source, parts):
    groups = len(parts[0])
    spots = [p[0].shape[0] for p in parts]
    rows = math.gcd(*spots)
    spots = [n // rows for n in spots]
    vmem = pl.BlockSpec(memory_space=pltpu.VMEM)
    columns = groups * sum(spots) * HEAD_DIM
    return pl.pallas_call(
        functools.partial(unpack_kernel, groups, spots, len(parts)),
        out_shape=jax.ShapeDtypeStruct((rows, columns), parts[0][0].dtype),
        in_specs=[pl.BlockSpec(memory_space=pltpu.SMEM)] + [vmem] * (groups * len(parts)),
        out_specs=vmem,
        cost_estimate=pl.CostEstimate(flops=0, transcendentals=0, bytes_accessed=4 * rows * columns),
    )(source, *[x for p in parts for x in p])


def dot(a, b, dims):
    return lax.dot_general(a, b, (dims, ((), ())), preferred_element_type=jnp.float32)


NN = ((1,), (0,))
NT = ((1,), (1,))


def head_kernel(kt, qt, count_ref, start_ref, target_ref, x_ref, d_ref, *rest):
    dq_refs, (s_ref, p_ref, dq_ref) = rest[:-3], rest[-3:]
    groups = x_ref.shape[0]
    count = count_ref[0]
    start = start_ref[0]
    scale = HEAD_DIM ** (-0.5)
    factor = scale * math.log2(math.e)
    q = x_ref[:, 2 * kt : 2 * kt + qt, :].reshape(groups * qt, HEAD_DIM)
    g = x_ref[:, 2 * kt + qt : 2 * kt + 2 * qt, :].reshape(groups * qt, HEAD_DIM)
    q_pos = start + lax.broadcasted_iota(jnp.int32, g.shape, 0)
    g = jnp.where(q_pos < count, g.astype(jnp.float32), 0.0).astype(g.dtype)
    slab = q.shape[0]
    top = jnp.full((8, slab), -jnp.inf, jnp.float32)
    for c in range(groups):
        s = dot(x_ref[c, :kt, :], q, NT) * factor
        k_pos = c * kt + lax.broadcasted_iota(jnp.int32, s.shape, 0)
        s = jnp.where(k_pos < count, s, -1e30)
        s_ref[c] = s
        top = jnp.maximum(top, jnp.max(s.reshape(kt // 8, 8, slab), axis=0))
    top = jnp.max(top, axis=0, keepdims=True)
    total = jnp.zeros((8, slab), jnp.float32)
    row_dot = jnp.zeros((8, slab), jnp.float32)
    for c in range(groups):
        e = jnp.exp2(s_ref[c] - top)
        s_ref[c] = e
        gp = dot(x_ref[c, kt : 2 * kt, :], g, NT)
        p_ref[c] = gp
        total += jnp.sum(e.reshape(kt // 8, 8, slab), axis=0)
        row_dot += jnp.sum((e * gp).reshape(kt // 8, 8, slab), axis=0)
    inv = 1.0 / jnp.sum(total, axis=0, keepdims=True)
    row_dot = jnp.sum(row_dot, axis=0, keepdims=True) * inv
    dq_t = jnp.zeros((HEAD_DIM, slab), jnp.float32)
    for c in range(groups):
        w = s_ref[c] * inv
        ds = (w * (p_ref[c] - row_dot)).astype(jnp.bfloat16)
        rows = pl.ds(c * kt, kt)
        d_ref[rows, :HEAD_DIM] = (dot(ds, q, NN) * scale).astype(d_ref.dtype)
        d_ref[rows, HEAD_DIM:] = dot(w.astype(jnp.bfloat16), g, NN).astype(d_ref.dtype)
        dq_t += dot(x_ref[c, :kt, :].T, ds, NN)
    dq_ref[...] = (dq_t * scale).T.reshape(dq_ref.shape)
    for k in range(groups):
        dq_refs[k][...] = dq_ref[target_ref[k]].astype(dq_refs[k].dtype)


def head_grads(x, token_counts, slab_start, target, kt, qt):
    groups = x.shape[0]
    keys, slab, rows = groups * kt, groups * qt, 2 * kt + 2 * qt
    heads = x.shape[1] // rows
    smem = pl.BlockSpec(memory_space=pltpu.SMEM)
    out = pl.pallas_call(
        functools.partial(head_kernel, kt, qt),
        grid=(heads,),
        out_shape=[jax.ShapeDtypeStruct((keys, heads * 2 * HEAD_DIM), jnp.bfloat16)]
        + [jax.ShapeDtypeStruct((heads * qt, HEAD_DIM), jnp.bfloat16)] * groups,
        in_specs=[smem, smem, smem, pl.BlockSpec((groups, rows, HEAD_DIM), lambda n: (0, n, 0))],
        out_specs=[pl.BlockSpec((keys, 2 * HEAD_DIM), lambda n: (0, n))]
        + [pl.BlockSpec((qt, HEAD_DIM), lambda n: (n, 0))] * groups,
        scratch_shapes=[
            pltpu.VMEM((groups, kt, slab), jnp.float32),
            pltpu.VMEM((groups, kt, slab), jnp.float32),
            pltpu.VMEM((groups, qt, HEAD_DIM), jnp.float32),
        ],
        compiler_params=pltpu.CompilerParams(vmem_limit_bytes=VMEM_LIMIT),
        cost_estimate=pl.CostEstimate(
            flops=20 * heads * keys * slab * HEAD_DIM,
            transcendentals=heads * keys * slab,
            bytes_accessed=4 * x.size,
        ),
    )(token_counts, slab_start, target, x)
    return out[0], out[1:]


def project_kernel(low_ref, *refs):
    d_refs, out_ref = refs[:-1], refs[-1]
    rank = low_ref.shape[1]
    kt = low_ref.shape[2]
    low_half = lax.broadcasted_iota(jnp.int32, (rank // 8, 8, HEAD_DIM), 1) < 4
    first, second = [], []
    for d_ref in d_refs:
        for n in range(d_ref.shape[1] // (2 * HEAD_DIM)):
            acc = jnp.zeros((rank, 2 * HEAD_DIM), jnp.float32)
            for c in range(low_ref.shape[0]):
                part = d_ref[c * kt : (c + 1) * kt, n * 2 * HEAD_DIM : (n + 1) * 2 * HEAD_DIM]
                acc += dot(low_ref[c], part, NN)
            wk = acc[:, :HEAD_DIM].reshape(rank // 8, 8, HEAD_DIM)
            wv = acc[:, HEAD_DIM:].reshape(rank // 8, 8, HEAD_DIM)
            first.append(jnp.where(low_half, wk, pltpu.roll(wv, 4, 1)))
            second.append(jnp.where(low_half, pltpu.roll(wk, 4, 1), wv))
    out_ref[:, 0] = jnp.concatenate(first, axis=1).astype(out_ref.dtype)
    out_ref[:, 1] = jnp.concatenate(second, axis=1).astype(out_ref.dtype)


def project(low_t, parts):
    rank = low_t.shape[1]
    vmem = pl.BlockSpec(memory_space=pltpu.VMEM)
    heads = sum(p.shape[1] for p in parts) // (2 * HEAD_DIM)
    out = pl.pallas_call(
        project_kernel,
        out_shape=jax.ShapeDtypeStruct((rank // 8, 2, heads * 8, HEAD_DIM), jnp.bfloat16),
        in_specs=[vmem] * (1 + len(parts)),
        out_specs=vmem,
        compiler_params=pltpu.CompilerParams(vmem_limit_bytes=VMEM_LIMIT),
        cost_estimate=pl.CostEstimate(
            flops=2 * rank * sum(p.size for p in parts),
            transcendentals=0,
            bytes_accessed=2 * sum(p.size for p in parts),
        ),
    )(low_t, *parts)
    return out.reshape(rank // 4, heads * 8, HEAD_DIM)


def shifted(index, k, groups, sign):
    ring = groups // 2
    half, place = index // ring, index % ring
    return (half + k // ring) % 2 * ring + (place + sign * (k % ring) + ring) % ring


def body(queries, keys, values, out_grad, layer_input, projection, token_counts, slab_start):
    groups = lax.axis_size("seq")
    clips = lax.axis_size("dp")
    kt, qt = keys.shape[1], queries.shape[1]
    heads = keys.shape[2] // HEAD_DIM // groups
    me = lax.axis_index("seq")
    ways = jnp.arange(groups, dtype=jnp.int32)
    target = shifted(me, ways, groups, 1)
    source = shifted(me, ways, groups, -1)

    pieces = ((0, 1), (2, 3), (4,))
    packed = pack(keys[0], values[0], queries[0], out_grad[0], pieces, groups)
    received = [lax.all_to_all(part, "seq", split_axis=0, concat_axis=0, tiled=True) for part in packed]

    low = jnp.dot(layer_input[0], projection, preferred_element_type=jnp.float32).astype(jnp.bfloat16)
    low_t = lax.all_gather(low.T, "seq", axis=0, tiled=False)

    grads, dq = [], []
    for part in received:
        d, dq_parts = head_grads(part, token_counts, slab_start, target, kt, qt)
        grads.append(d)
        dq.append(dq_parts)

    dq = [[jnp.concatenate(x, axis=0) for x in zip(*dq[:-1])], dq[-1]]
    back = [
        [p[0]]
        + [
            lax.ppermute(p[k], "seq", [(i, shifted(i, k, groups, 1)) for i in range(groups)])
            for k in range(1, groups)
        ]
        for p in dq
    ]
    query_grad = unpack(source, back)[None]

    got = lax.all_to_all(project(low_t, grads), ("dp", "seq"), split_axis=0, concat_axis=0, tiled=True)
    got = got.reshape(clips, groups, heads, 2, 4, HEAD_DIM).astype(jnp.float32)
    total = jnp.sum(got, axis=0) * (1.0 / clips)
    projected = jnp.transpose(total, (3, 2, 0, 1, 4)).reshape(4, 2, groups * heads * HEAD_DIM)
    return (query_grad, projected)


def solution(mesh):
    return jax.shard_map(
        body,
        mesh=mesh,
        in_specs=(
            P("dp", "seq", None),
            P("dp", "seq", None),
            P("dp", "seq", None),
            P("dp", "seq", None),
            P("dp", "seq", None),
            P(),
            P("dp"),
            P("dp"),
        ),
        out_specs=(P("dp", "seq", None), P(("dp", "seq"), None, None)),
        check_vma=False,
    )
```

```python
import functools
import math

import jax
import jax.numpy as jnp
from jax import lax
from jax.experimental import pallas as pl
from jax.experimental.pallas import tpu as pltpu
from jax.sharding import PartitionSpec as P

HEAD_DIM = 128
VMEM_LIMIT = 60 * 1024 * 1024
DP_PAIRS = 8


def pack_kernel(pieces, *refs):
    ins, outs = iter(refs[: -len(pieces)]), refs[-len(pieces) :]
    for heads, out in zip(pieces, outs):
        row = 0
        for src in [next(ins) for _ in range(4 * len(heads))]:
            rows = src.shape[0]
            out[0, row : row + rows, :] = src[...]
            row += rows


def pack(arrays, pieces, groups):
    width = arrays[0].shape[1]
    rows = sum(x.shape[0] for x in arrays)
    per_group = width // HEAD_DIM // groups
    heads = [head for piece in pieces for head in piece]
    return pl.pallas_call(
        functools.partial(pack_kernel, pieces),
        grid=(groups,),
        out_shape=[jax.ShapeDtypeStruct((groups, len(p) * rows, HEAD_DIM), arrays[0].dtype) for p in pieces],
        in_specs=[
            pl.BlockSpec((x.shape[0], HEAD_DIM), lambda j, head=head: (0, j * per_group + head))
            for head in heads
            for x in arrays
        ],
        out_specs=[pl.BlockSpec((1, len(p) * rows, HEAD_DIM), lambda j: (j, 0, 0)) for p in pieces],
        compiler_params=pltpu.CompilerParams(vmem_limit_bytes=VMEM_LIMIT),
        cost_estimate=pl.CostEstimate(
            flops=0, transcendentals=0, bytes_accessed=4 * len(heads) * groups * rows * HEAD_DIM
        ),
    )(*[x for _ in heads for x in arrays])


def unpack_kernel(per_group, source_ref, *refs):
    ins, out_ref = refs[:-1], refs[-1]
    rows = out_ref.shape[0]
    for k, src in enumerate(ins):
        for head in range(per_group):
            column = pl.multiple_of((source_ref[k] * per_group + head) * HEAD_DIM, HEAD_DIM)
            out_ref[:, pl.ds(column, HEAD_DIM)] = src[head * rows : (head + 1) * rows, :]


def unpack(source, parts, rows):
    vmem = pl.BlockSpec(memory_space=pltpu.VMEM)
    per_group = parts[0].shape[0] // rows
    columns = len(parts) * per_group * HEAD_DIM
    return pl.pallas_call(
        functools.partial(unpack_kernel, per_group),
        out_shape=jax.ShapeDtypeStruct((rows, columns), parts[0].dtype),
        in_specs=[pl.BlockSpec(memory_space=pltpu.SMEM)] + [vmem] * len(parts),
        out_specs=vmem,
        compiler_params=pltpu.CompilerParams(vmem_limit_bytes=VMEM_LIMIT),
        cost_estimate=pl.CostEstimate(flops=0, transcendentals=0, bytes_accessed=4 * rows * columns),
    )(source, *parts)


def dot(a, b, dims):
    return lax.dot_general(a, b, (dims, ((), ())), preferred_element_type=jnp.float32)


NN = ((1,), (0,))
NT = ((1,), (1,))


def head_kernel(kt, qt, ways, ndq, count_ref, start_ref, target_ref, source_ref, core_ref, x_ref, *rest):
    nlow = len(ways)
    low_refs, early_dq, rest = rest[:nlow], rest[nlow : nlow + ndq], rest[nlow + ndq :]
    if nlow:
        keep_ref, give_ref, rest = rest[0], rest[1], rest[2:]
    else:
        d_ref, rest = rest[0], rest[1:]
    dq_refs, scratch = rest[:x_ref.shape[0]], rest[x_ref.shape[0]:]
    s_ref, p_ref, dq_ref = scratch[:3]
    if nlow:
        d_ref = scratch[3]
    groups = x_ref.shape[0]
    count = count_ref[0]
    start = start_ref[0]
    scale = HEAD_DIM ** (-0.5)
    factor = scale * math.log2(math.e)
    q = x_ref[:, 2 * kt : 2 * kt + qt, :].reshape(groups * qt, HEAD_DIM)
    g = x_ref[:, 2 * kt + qt : 2 * kt + 2 * qt, :].reshape(groups * qt, HEAD_DIM)
    q_pos = start + lax.broadcasted_iota(jnp.int32, g.shape, 0)
    g = jnp.where(q_pos < count, g.astype(jnp.float32), 0.0).astype(g.dtype)
    slab = q.shape[0]
    top = jnp.full((8, slab), -jnp.inf, jnp.float32)
    for c in range(groups):
        s = dot(x_ref[c, :kt, :], q, NT) * factor
        k_pos = c * kt + lax.broadcasted_iota(jnp.int32, s.shape, 0)
        s = jnp.where(k_pos < count, s, -1e30)
        s_ref[c] = s
        top = jnp.maximum(top, jnp.max(s.reshape(kt // 8, 8, slab), axis=0))
    top = jnp.max(top, axis=0, keepdims=True)
    total = jnp.zeros((8, slab), jnp.float32)
    row_dot = jnp.zeros((8, slab), jnp.float32)
    for c in range(groups):
        e = jnp.exp2(s_ref[c] - top)
        s_ref[c] = e
        gp = dot(x_ref[c, kt : 2 * kt, :], g, NT)
        p_ref[c] = gp
        total += jnp.sum(e.reshape(kt // 8, 8, slab), axis=0)
        row_dot += jnp.sum((e * gp).reshape(kt // 8, 8, slab), axis=0)
    inv = 1.0 / jnp.sum(total, axis=0, keepdims=True)
    row_dot = jnp.sum(row_dot, axis=0, keepdims=True) * inv
    dq_t = jnp.zeros((HEAD_DIM, slab), jnp.float32)
    for c in range(groups):
        w = s_ref[c] * inv
        ds = (w * (p_ref[c] - row_dot)).astype(jnp.bfloat16)
        rows = pl.ds(c * kt, kt)
        d_ref[rows, :HEAD_DIM] = (dot(ds, q, NN) * scale).astype(d_ref.dtype)
        d_ref[rows, HEAD_DIM:] = dot(w.astype(jnp.bfloat16), g, NN).astype(d_ref.dtype)
        dq_t += dot(x_ref[c, :kt, :].T, ds, NN)
    dq_ref[...] = (dq_t * scale).T.reshape(dq_ref.shape)
    for k in range(groups):
        row = 0
        for ref in early_dq[k::groups]:
            dq_refs[k][row : row + ref.shape[0], :] = ref[...]
            row += ref.shape[0]
        dq_refs[k][row : row + qt, :] = dq_ref[target_ref[k]].astype(dq_refs[k].dtype)
    if nlow:
        keep, give = divide([spread(project_head(ways, low_refs, d_ref, source_ref))], core_ref)
        keep_ref[...] = keep.astype(keep_ref.dtype)
        give_ref[...] = give.astype(give_ref.dtype)


def project_head(ways, low_refs, d_ref, source_ref, column=0):
    _, rank, kt = low_refs[0].shape
    acc = jnp.zeros((rank, 2 * HEAD_DIM), jnp.float32)
    for way, low_ref in zip(ways, low_refs):
        for b, w in enumerate(way):
            row = pl.multiple_of(source_ref[w] * kt, kt)
            acc += dot(low_ref[b], d_ref[pl.ds(row, kt), column : column + 2 * HEAD_DIM], NN)
    return acc


def divide(parts, core_ref):
    w = jnp.concatenate(parts, axis=2) if len(parts) > 1 else parts[0]
    w = w.reshape(DP_PAIRS, 2, -1, *w.shape[1:])
    even = core_ref[0] == 0
    return jnp.where(even, w[:, 0], w[:, 1]), jnp.where(even, w[:, 1], w[:, 0])


def spread(acc):
    tiles = acc.shape[0] // 8
    low_half = lax.broadcasted_iota(jnp.int32, (tiles, 8, HEAD_DIM), 1) < 4
    wk = acc[:, :HEAD_DIM].reshape(tiles, 8, HEAD_DIM)
    wv = acc[:, HEAD_DIM:].reshape(tiles, 8, HEAD_DIM)
    first = jnp.where(low_half, wk, pltpu.roll(wv, 4, 1))
    second = jnp.where(low_half, pltpu.roll(wk, 4, 1), wv)
    return jnp.stack([first, second], axis=1)


def head_grads(x, scalars, kt, qt, low=(), ways=(), early_dq=()):
    groups = x.shape[0]
    keys, slab, rows = groups * kt, groups * qt, 2 * kt + 2 * qt
    heads = x.shape[1] // rows
    smem = pl.BlockSpec(memory_space=pltpu.SMEM)
    scratch = [
        pltpu.VMEM((groups, kt, slab), jnp.float32),
        pltpu.VMEM((groups, kt, slab), jnp.float32),
        pltpu.VMEM((groups, qt, HEAD_DIM), jnp.float32),
    ]
    if low:
        first = [split_shape(low[0].shape[1], 1)] * 2
        first_spec = [pl.BlockSpec(e.shape, lambda n, rank=len(e.shape): (0,) * rank) for e in first]
        scratch.append(pltpu.VMEM((keys, 2 * HEAD_DIM), jnp.bfloat16))
    else:
        first = [jax.ShapeDtypeStruct((keys, heads * 2 * HEAD_DIM), jnp.bfloat16)]
        first_spec = [pl.BlockSpec((keys, 2 * HEAD_DIM), lambda n: (0, n))]
    before = [p for parts in early_dq for p in parts]
    extra = list(low) + before
    dq_rows = qt + sum(parts[0].shape[0] for parts in early_dq)
    out = pl.pallas_call(
        functools.partial(head_kernel, kt, qt, ways, len(before)),
        grid=(heads,),
        out_shape=first + [jax.ShapeDtypeStruct((heads * dq_rows, HEAD_DIM), jnp.bfloat16)] * groups,
        in_specs=[smem] * len(scalars)
        + [pl.BlockSpec((groups, rows, HEAD_DIM), lambda n: (0, n, 0))]
        + [pl.BlockSpec(e.shape, lambda n, rank=e.ndim: (0,) * rank) for e in extra],
        out_specs=first_spec + [pl.BlockSpec((dq_rows, HEAD_DIM), lambda n: (n, 0))] * groups,
        scratch_shapes=scratch,
        compiler_params=pltpu.CompilerParams(vmem_limit_bytes=VMEM_LIMIT),
        cost_estimate=pl.CostEstimate(
            flops=20 * heads * keys * slab * HEAD_DIM,
            transcendentals=heads * keys * slab,
            bytes_accessed=4 * x.size,
        ),
    )(*scalars, x, *extra)
    return out[: len(first)], out[len(first) :]


def split_shape(rank, heads):
    return jax.ShapeDtypeStruct((DP_PAIRS, rank // 16 // DP_PAIRS, 2, 8 * heads, HEAD_DIM), jnp.bfloat16)


def project_kernel(ways, source_ref, core_ref, *refs):
    low_refs, d_ref, out_ref, give_ref = refs[:-3], refs[-3], refs[-2], refs[-1]
    columns = range(0, d_ref.shape[1], 2 * HEAD_DIM)
    parts = [spread(project_head(ways, low_refs, d_ref, source_ref, column)) for column in columns]
    keep, give = divide(parts, core_ref)
    out_ref[...] = keep.astype(out_ref.dtype)
    give_ref[...] = give.astype(give_ref.dtype)


def project(low, ways, scalars, part):
    rank = low[0].shape[1]
    out = split_shape(rank, part.shape[1] // (2 * HEAD_DIM))
    vmem = pl.BlockSpec(memory_space=pltpu.VMEM)
    return pl.pallas_call(
        functools.partial(project_kernel, ways),
        out_shape=[out] * 2,
        in_specs=[pl.BlockSpec(memory_space=pltpu.SMEM)] * 2 + [vmem] * (len(low) + 1),
        out_specs=[vmem] * 2,
        compiler_params=pltpu.CompilerParams(vmem_limit_bytes=VMEM_LIMIT),
        cost_estimate=pl.CostEstimate(
            flops=2 * rank * part.size, transcendentals=0, bytes_accessed=4 * part.size
        ),
    )(*scalars[-2:], *low, part)


def shifted(index, k, groups, sign):
    ring = groups // 2
    half, place = index // ring, index % ring
    return (half + k // ring) % 2 * ring + (place + sign * (k % ring) + ring) % ring


def body(queries, keys, values, out_grad, layer_input, projection, token_counts, slab_start):
    groups = lax.axis_size("seq")
    clips = lax.axis_size("dp")
    kt, qt = keys.shape[1], queries.shape[1]
    heads = keys.shape[2] // HEAD_DIM // groups
    me = lax.axis_index("seq")
    ways = jnp.arange(groups, dtype=jnp.int32)
    target = shifted(me, ways, groups, 1)
    source = shifted(me, ways, groups, -1)

    def send(x, k):
        return lax.ppermute(x, "seq", [(i, shifted(i, k, groups, 1)) for i in range(groups)])

    def exchange(x):
        return lax.all_to_all(x, "seq", split_axis=0, concat_axis=0, tiled=True)

    def after(x, *others):
        return lax.optimization_barrier((x, *others))

    clip = lax.axis_index("dp")
    scalars = (token_counts, slab_start, target, source, (clip % 2).reshape(1))

    def attend(part, *more):
        return head_grads(part, scalars, kt, qt, *more)

    def other_core(x):
        return lax.ppermute(x, "dp", [(i, i ^ 1) for i in range(clips)])

    arrays = (keys[0], values[0], queries[0], out_grad[0])
    low = jnp.dot(layer_input[0], projection, preferred_element_type=jnp.float32).astype(jnp.bfloat16).T
    arrays, low = after(arrays, low)
    ring = groups // 2
    pair = jnp.stack([low, send(low, ring)])
    part0, = pack(arrays, ((0, 1),), groups)
    part0, pair = after(part0, pair)
    left, right = send(pair, 1), send(pair, ring - 1)
    ways = ((0, ring), (1, ring + 1), (ring - 1, 2 * ring - 1), (2,), (ring + 2,))
    got0 = exchange(part0)
    arrays, part0 = after(arrays, part0)
    part1, part2 = pack(arrays, ((2, 3), (4,)), groups)

    part1, got0, left, right = after(part1, got0, left, right)
    low = [pair, left, right, send(left[:1], 1), send(right[1:], ring - 1)]
    got1 = exchange(part1)
    (d0,), dq0 = attend(got0)
    part2, got1, d0, low = after(part2, got1, d0, low)
    sums = [project(low, ways, scalars, d0)]
    got2 = exchange(part2)
    (d1,), dq1 = attend(got1)
    sums.append(project(low, ways, scalars, d1))
    late, dq = attend(got2, low, ways, [dq0, dq1])
    sums.append(late)

    back = [dq[0]] + [send(dq[k], k) for k in range(1, groups)]
    query_grad = unpack(source, back, qt)[None]
    pairs = [keep.astype(jnp.float32) + other_core(give).astype(jnp.float32) for keep, give in sums]
    mine = jnp.concatenate(pairs, axis=3).astype(jnp.bfloat16).reshape(-1, heads * 8, HEAD_DIM)
    alike = [
        [i * groups + j for i in range(core, clips, 2) for j in range(groups)] for core in range(2)
    ]
    got = lax.all_to_all(
        mine, ("dp", "seq"), split_axis=0, concat_axis=0, axis_index_groups=alike, tiled=True
    )
    got = got.reshape(clips // 2, groups, heads, 2, 4, HEAD_DIM).astype(jnp.float32)
    total = jnp.sum(got, axis=0) * (1.0 / clips)
    projected = jnp.transpose(total, (3, 2, 0, 1, 4)).reshape(4, 2, groups * heads * HEAD_DIM)
    return (query_grad, projected)


def solution(mesh):
    return jax.shard_map(
        body,
        mesh=mesh,
        in_specs=(
            P("dp", "seq", None),
            P("dp", "seq", None),
            P("dp", "seq", None),
            P("dp", "seq", None),
            P("dp", "seq", None),
            P(),
            P("dp"),
            P("dp"),
        ),
        out_specs=(P("dp", "seq", None), P(("dp", "seq"), None, None)),
        check_vma=False,
    )
```

```python
import functools
import math

import jax
import jax.numpy as jnp
from jax import lax
from jax.experimental import pallas as pl
from jax.experimental.pallas import tpu as pltpu
from jax.sharding import PartitionSpec as P

HEAD_DIM = 128
VMEM_LIMIT = 60 * 1024 * 1024
DP_PAIRS = 8


def pack_kernel(pieces, groups, with_low, *refs):
    sources, refs = refs[:4], refs[4:]
    if with_low:
        low_ref, refs = refs[0], refs[1:]
    n = len(pieces)
    outs, bufs, in_sem, out_sem, refs = refs[:n], refs[n : 2 * n], refs[2 * n], refs[2 * n + 1], refs[2 * n + 2 :]
    per_group = sources[0].shape[1] // HEAD_DIM // groups
    loads, low_loads, stores = {}, [], []
    count = 0
    if with_low:
        low_buf, low_sem = refs
        rank = low_ref.shape[0]
        for b in range(low_ref.shape[1] // HEAD_DIM):
            columns = pl.ds(b * HEAD_DIM, HEAD_DIM)
            copy = pltpu.make_async_copy(low_ref.at[:, columns], low_buf.at[pl.ds(b * rank, rank), :], low_sem.at[b])
            copy.start()
            low_loads.append(copy)
    for p, heads in enumerate(pieces):
        for j in range(groups):
            row = 0
            loads[p, j] = []
            for head in heads:
                for src in sources:
                    rows = src.shape[0]
                    columns = pl.ds((j * per_group + head) * HEAD_DIM, HEAD_DIM)
                    copy = pltpu.make_async_copy(
                        src.at[:, columns], bufs[p].at[j, pl.ds(row, rows), :], in_sem.at[count]
                    )
                    copy.start()
                    loads[p, j].append(copy)
                    count += 1
                    row += rows

    def store(src, dst):
        copy = pltpu.make_async_copy(src, dst, out_sem.at[len(stores)])
        copy.start()
        stores.append(copy)

    for copy in low_loads:
        copy.wait()
    for p in range(n):
        rows = bufs[p].shape[1]
        for j in range(groups):
            for copy in loads[p, j]:
                copy.wait()
            store(bufs[p].at[j], outs[p].at[j, pl.ds(0, rows), :])
            if with_low and p == 0:
                store(low_buf, outs[p].at[j, pl.ds(rows, low_buf.shape[0]), :])
    for copy in stores:
        copy.wait()


def pack(arrays, pieces, groups, low=None):
    rows = sum(x.shape[0] for x in arrays)
    heads = sum(len(p) for p in pieces)
    hbm = pl.BlockSpec(memory_space=pl.ANY)
    shapes = [(groups, len(p) * rows, HEAD_DIM) for p in pieces]
    outs = list(shapes)
    scratch = [pltpu.VMEM(e, arrays[0].dtype) for e in shapes] + [
        pltpu.SemaphoreType.DMA((len(arrays) * groups * heads,)),
        pltpu.SemaphoreType.DMA((groups * (len(pieces) + 1),)),
    ]
    if low is not None:
        low_rows = low.size // HEAD_DIM
        outs[0] = (groups, shapes[0][1] + low_rows, HEAD_DIM)
        scratch += [
            pltpu.VMEM((low_rows, HEAD_DIM), low.dtype),
            pltpu.SemaphoreType.DMA((low.shape[1] // HEAD_DIM,)),
        ]
        arrays = (*arrays, low)
    return pl.pallas_call(
        functools.partial(pack_kernel, pieces, groups, low is not None),
        out_shape=[jax.ShapeDtypeStruct(e, arrays[0].dtype) for e in outs],
        in_specs=[hbm] * len(arrays),
        out_specs=[hbm] * len(pieces),
        scratch_shapes=scratch,
        compiler_params=pltpu.CompilerParams(vmem_limit_bytes=VMEM_LIMIT),
        cost_estimate=pl.CostEstimate(
            flops=0, transcendentals=0, bytes_accessed=4 * heads * groups * rows * HEAD_DIM
        ),
    )(*arrays)


def unpack_kernel(per_group, source_ref, *refs):
    ins, out_ref = refs[:-1], refs[-1]
    rows = out_ref.shape[0]
    for k, src in enumerate(ins):
        for head in range(per_group):
            column = pl.multiple_of((source_ref[k] * per_group + head) * HEAD_DIM, HEAD_DIM)
            out_ref[:, pl.ds(column, HEAD_DIM)] = src[head * rows : (head + 1) * rows, :]


def unpack(source, parts, rows):
    vmem = pl.BlockSpec(memory_space=pltpu.VMEM)
    per_group = parts[0].shape[0] // rows
    columns = len(parts) * per_group * HEAD_DIM
    return pl.pallas_call(
        functools.partial(unpack_kernel, per_group),
        out_shape=jax.ShapeDtypeStruct((rows, columns), parts[0].dtype),
        in_specs=[pl.BlockSpec(memory_space=pltpu.SMEM)] + [vmem] * len(parts),
        out_specs=vmem,
        compiler_params=pltpu.CompilerParams(vmem_limit_bytes=VMEM_LIMIT),
        cost_estimate=pl.CostEstimate(flops=0, transcendentals=0, bytes_accessed=4 * rows * columns),
    )(source, *parts)


def dot(a, b, dims):
    return lax.dot_general(a, b, (dims, ((), ())), preferred_element_type=jnp.float32)


NN = ((1,), (0,))
NT = ((1,), (1,))


def head_kernel(kt, qt, nlow, nprior, ndq, count_ref, start_ref, target_ref, core_ref, x_ref, *rest):
    low_refs, prior_refs, rest = rest[:nlow], rest[nlow : nlow + nprior], rest[nlow + nprior :]
    early_dq, rest = rest[:ndq], rest[ndq:]
    if nlow:
        keep_ref, give_ref, rest = rest[0], rest[1], rest[2:]
    else:
        d_ref, rest = rest[0], rest[1:]
    dq_refs, scratch = rest[:x_ref.shape[0]], rest[x_ref.shape[0]:]
    s_ref, p_ref, dq_ref = scratch[:3]
    if nlow:
        d_ref, full_ref, low_sem, prior_sem = scratch[3:7]
        bufs = scratch[7:]
        copies = gather_low(2 * kt + 2 * qt, low_refs[0], full_ref, low_sem)
        for n in range(nprior):
            copies.append(pltpu.make_async_copy(prior_refs[n], bufs[n], prior_sem.at[n]))
            copies[-1].start()
    groups = x_ref.shape[0]
    count = count_ref[0]
    start = start_ref[0]
    scale = HEAD_DIM ** (-0.5)
    factor = scale * math.log2(math.e)
    q = x_ref[:, 2 * kt : 2 * kt + qt, :].reshape(groups * qt, HEAD_DIM)
    g = x_ref[:, 2 * kt + qt : 2 * kt + 2 * qt, :].reshape(groups * qt, HEAD_DIM)
    q_pos = start + lax.broadcasted_iota(jnp.int32, g.shape, 0)
    g = jnp.where(q_pos < count, g.astype(jnp.float32), 0.0).astype(g.dtype)
    slab = q.shape[0]
    top = jnp.full((8, slab), -jnp.inf, jnp.float32)
    for c in range(groups):
        s = dot(x_ref[c, :kt, :], q, NT) * factor
        k_pos = c * kt + lax.broadcasted_iota(jnp.int32, s.shape, 0)
        s = jnp.where(k_pos < count, s, -1e30)
        s_ref[c] = s
        top = jnp.maximum(top, jnp.max(s.reshape(kt // 8, 8, slab), axis=0))
    top = jnp.max(top, axis=0, keepdims=True)
    total = jnp.zeros((8, slab), jnp.float32)
    row_dot = jnp.zeros((8, slab), jnp.float32)
    for c in range(groups):
        e = jnp.exp2(s_ref[c] - top)
        s_ref[c] = e
        gp = dot(x_ref[c, kt : 2 * kt, :], g, NT)
        p_ref[c] = gp
        total += jnp.sum(e.reshape(kt // 8, 8, slab), axis=0)
        row_dot += jnp.sum((e * gp).reshape(kt // 8, 8, slab), axis=0)
    inv = 1.0 / jnp.sum(total, axis=0, keepdims=True)
    row_dot = jnp.sum(row_dot, axis=0, keepdims=True) * inv
    dq_t = jnp.zeros((HEAD_DIM, slab), jnp.float32)
    for c in range(groups):
        w = s_ref[c] * inv
        ds = (w * (p_ref[c] - row_dot)).astype(jnp.bfloat16)
        rows = pl.ds(c * kt, kt)
        d_ref[rows, :HEAD_DIM] = (dot(ds, q, NN) * scale).astype(d_ref.dtype)
        d_ref[rows, HEAD_DIM:] = dot(w.astype(jnp.bfloat16), g, NN).astype(d_ref.dtype)
        dq_t += dot(x_ref[c, :kt, :].T, ds, NN)
    dq_ref[...] = (dq_t * scale).T.reshape(dq_ref.shape)
    for k in range(groups):
        row = 0
        for ref in early_dq[k::groups]:
            dq_refs[k][row : row + ref.shape[0], :] = ref[...]
            row += ref.shape[0]
        dq_refs[k][row : row + qt, :] = dq_ref[target_ref[k]].astype(dq_refs[k].dtype)
    if nlow:
        for copy in copies:
            copy.wait()
        results = []
        for ref in (*bufs, d_ref):
            for column in range(0, ref.shape[1], 2 * HEAD_DIM):
                part = ref[:, column : column + 2 * HEAD_DIM]
                results.append(spread(dot(full_ref[...], part, NN)))
        keep, give = divide(results, core_ref)
        keep_ref[...] = keep.astype(keep_ref.dtype)
        give_ref[...] = give.astype(give_ref.dtype)


def gather_low(first, low_ref, full_ref, sem):
    rank = full_ref.shape[0]
    copies = []
    for j in range(low_ref.shape[0]):
        for row in range(first, low_ref.shape[1], rank):
            columns = pl.ds(len(copies) * HEAD_DIM, HEAD_DIM)
            copy = pltpu.make_async_copy(
                low_ref.at[j, pl.ds(row, rank), :], full_ref.at[:, columns], sem.at[len(copies)]
            )
            copy.start()
            copies.append(copy)
    return copies


def divide(parts, core_ref):
    w = jnp.concatenate(parts, axis=2) if len(parts) > 1 else parts[0]
    w = w.reshape(DP_PAIRS, 2, -1, *w.shape[1:])
    even = core_ref[0] == 0
    return jnp.where(even, w[:, 0], w[:, 1]), jnp.where(even, w[:, 1], w[:, 0])


def spread(acc):
    tiles = acc.shape[0] // 8
    low_half = lax.broadcasted_iota(jnp.int32, (tiles, 8, HEAD_DIM), 1) < 4
    wk = acc[:, :HEAD_DIM].reshape(tiles, 8, HEAD_DIM)
    wv = acc[:, HEAD_DIM:].reshape(tiles, 8, HEAD_DIM)
    first = jnp.where(low_half, wk, pltpu.roll(wv, 4, 1))
    second = jnp.where(low_half, pltpu.roll(wk, 4, 1), wv)
    return jnp.stack([first, second], axis=1)


def head_grads(x, heads, scalars, kt, qt, rank, low=(), prior=(), early_dq=()):
    groups = x.shape[0]
    keys, slab, rows = groups * kt, groups * qt, 2 * kt + 2 * qt
    smem = pl.BlockSpec(memory_space=pltpu.SMEM)
    scratch = [
        pltpu.VMEM((groups, kt, slab), jnp.float32),
        pltpu.VMEM((groups, kt, slab), jnp.float32),
        pltpu.VMEM((groups, qt, HEAD_DIM), jnp.float32),
    ]
    if low:
        first = [split_shape(rank, 1 + sum(p.shape[1] for p in prior) // (2 * HEAD_DIM))] * 2
        first_spec = [pl.BlockSpec(e.shape, lambda n, rank=len(e.shape): (0,) * rank) for e in first]
        scratch += [
            pltpu.VMEM((keys, 2 * HEAD_DIM), jnp.bfloat16),
            pltpu.VMEM((rank, keys), jnp.bfloat16),
            pltpu.SemaphoreType.DMA((keys // HEAD_DIM,)),
            pltpu.SemaphoreType.DMA((len(prior),)),
        ] + [pltpu.VMEM(p.shape, p.dtype) for p in prior]
    else:
        first = [jax.ShapeDtypeStruct((keys, heads * 2 * HEAD_DIM), jnp.bfloat16)]
        first_spec = [pl.BlockSpec((keys, 2 * HEAD_DIM), lambda n: (0, n))]
    before = [p for parts in early_dq for p in parts]
    dq_rows = qt + sum(parts[0].shape[0] for parts in early_dq)
    out = pl.pallas_call(
        functools.partial(head_kernel, kt, qt, len(low), len(prior), len(before)),
        grid=(heads,),
        out_shape=first + [jax.ShapeDtypeStruct((heads * dq_rows, HEAD_DIM), jnp.bfloat16)] * groups,
        in_specs=[smem] * len(scalars)
        + [pl.BlockSpec((groups, rows, HEAD_DIM), lambda n: (0, n, 0))]
        + [pl.BlockSpec(memory_space=pl.ANY)] * (len(low) + len(prior))
        + [pl.BlockSpec(e.shape, lambda n, rank=e.ndim: (0,) * rank) for e in before],
        out_specs=first_spec + [pl.BlockSpec((dq_rows, HEAD_DIM), lambda n: (n, 0))] * groups,
        scratch_shapes=scratch,
        compiler_params=pltpu.CompilerParams(vmem_limit_bytes=VMEM_LIMIT),
        cost_estimate=pl.CostEstimate(
            flops=20 * heads * keys * slab * HEAD_DIM,
            transcendentals=heads * keys * slab,
            bytes_accessed=4 * x.size,
        ),
    )(*scalars, x, *low, *prior, *before)
    return out[: len(first)], out[len(first) :]


def split_shape(rank, heads):
    return jax.ShapeDtypeStruct((DP_PAIRS, rank // 16 // DP_PAIRS, 2, 8 * heads, HEAD_DIM), jnp.bfloat16)


def shifted(index, k, groups, sign):
    ring = groups // 2
    half, place = index // ring, index % ring
    return (half + k // ring) % 2 * ring + (place + sign * (k % ring) + ring) % ring


def body(queries, keys, values, out_grad, layer_input, projection, token_counts, slab_start):
    groups = lax.axis_size("seq")
    clips = lax.axis_size("dp")
    kt, qt = keys.shape[1], queries.shape[1]
    heads = keys.shape[2] // HEAD_DIM // groups
    me = lax.axis_index("seq")
    ways = jnp.arange(groups, dtype=jnp.int32)
    target = shifted(me, ways, groups, 1)
    source = shifted(me, ways, groups, -1)

    def send(x, k):
        return lax.ppermute(x, "seq", [(i, shifted(i, k, groups, 1)) for i in range(groups)])

    def exchange(x):
        return lax.all_to_all(x, "seq", split_axis=0, concat_axis=0, tiled=True)

    def after(x, *others):
        return lax.optimization_barrier((x, *others))

    clip = lax.axis_index("dp")
    scalars = (token_counts, slab_start, target, (clip % 2).reshape(1))

    rank = projection.shape[1]

    def attend(part, count, *more):
        return head_grads(part, count, scalars, kt, qt, rank, *more)

    def other_core(x):
        return lax.ppermute(x, "dp", [(i, i ^ 1) for i in range(clips)])

    first, second = tuple(range(heads - 1)), (heads - 1,)
    arrays = (keys[0], values[0], queries[0], out_grad[0])
    part0, = pack(arrays, (first,), groups)
    rest, part0 = after((arrays, layer_input), part0)
    arrays, layer_input = rest
    got0 = exchange(part0)
    low = jnp.dot(layer_input[0], projection, preferred_element_type=jnp.float32).astype(jnp.bfloat16).T
    part1, = pack(arrays, (second,), groups, low)
    part1, got0 = after(part1, got0)
    got1 = exchange(part1)
    d0, dq0 = attend(got0, len(first))
    (keep, give), dq = attend(got1, len(second), [got1], d0, [dq0])

    back = [dq[0]] + [send(dq[k], k) for k in range(1, groups)]
    query_grad = unpack(source, back, qt)[None]
    mine = (keep.astype(jnp.float32) + other_core(give).astype(jnp.float32)).astype(jnp.bfloat16)
    mine = mine.reshape(-1, heads * 8, HEAD_DIM)
    alike = [
        [i * groups + j for i in range(core, clips, 2) for j in range(groups)] for core in range(2)
    ]
    got = lax.all_to_all(
        mine, ("dp", "seq"), split_axis=0, concat_axis=0, axis_index_groups=alike, tiled=True
    )
    got = got.reshape(clips // 2, groups, heads, 2, 4, HEAD_DIM).astype(jnp.float32)
    total = jnp.sum(got, axis=0) * (1.0 / clips)
    projected = jnp.transpose(total, (3, 2, 0, 1, 4)).reshape(4, 2, groups * heads * HEAD_DIM)
    return (query_grad, projected)


def solution(mesh):
    return jax.shard_map(
        body,
        mesh=mesh,
        in_specs=(
            P("dp", "seq", None),
            P("dp", "seq", None),
            P("dp", "seq", None),
            P("dp", "seq", None),
            P("dp", "seq", None),
            P(),
            P("dp"),
            P("dp"),
        ),
        out_specs=(P("dp", "seq", None), P(("dp", "seq"), None, None)),
        check_vma=False,
    )
```

```python
import functools
import math

import jax
import jax.numpy as jnp
from jax import lax
from jax.experimental import pallas as pl
from jax.experimental.pallas import tpu as pltpu
from jax.sharding import PartitionSpec as P

HEAD_DIM = 128
VMEM_LIMIT = 60 * 1024 * 1024
DP_PAIRS = 8


def pack_kernel(pieces, groups, *refs):
    sources, refs = refs[:4], refs[4:]
    n = len(pieces)
    outs, bufs, in_sem, out_sem = refs[:n], refs[n : 2 * n], refs[2 * n], refs[2 * n + 1]
    per_group = sources[0].shape[1] // HEAD_DIM // groups
    loads, stores = {}, []
    count = 0
    for p, heads in enumerate(pieces):
        for j in range(groups):
            row = 0
            loads[p, j] = []
            for head in heads:
                for src in sources:
                    rows = src.shape[0]
                    columns = pl.ds((j * per_group + head) * HEAD_DIM, HEAD_DIM)
                    copy = pltpu.make_async_copy(
                        src.at[:, columns], bufs[p].at[j, pl.ds(row, rows), :], in_sem.at[count]
                    )
                    copy.start()
                    loads[p, j].append(copy)
                    count += 1
                    row += rows
    for p in range(n):
        for j in range(groups):
            for copy in loads[p, j]:
                copy.wait()
            copy = pltpu.make_async_copy(bufs[p].at[j], outs[p].at[j], out_sem.at[len(stores)])
            copy.start()
            stores.append(copy)
    for copy in stores:
        copy.wait()


def pack(arrays, pieces, groups):
    rows = sum(x.shape[0] for x in arrays)
    heads = sum(len(p) for p in pieces)
    hbm = pl.BlockSpec(memory_space=pl.ANY)
    shapes = [(groups, len(p) * rows, HEAD_DIM) for p in pieces]
    return pl.pallas_call(
        functools.partial(pack_kernel, pieces, groups),
        out_shape=[jax.ShapeDtypeStruct(e, arrays[0].dtype) for e in shapes],
        in_specs=[hbm] * len(arrays),
        out_specs=[hbm] * len(pieces),
        scratch_shapes=[pltpu.VMEM(e, arrays[0].dtype) for e in shapes]
        + [
            pltpu.SemaphoreType.DMA((len(arrays) * groups * heads,)),
            pltpu.SemaphoreType.DMA((groups * len(pieces),)),
        ],
        compiler_params=pltpu.CompilerParams(vmem_limit_bytes=VMEM_LIMIT),
        cost_estimate=pl.CostEstimate(
            flops=0, transcendentals=0, bytes_accessed=4 * heads * groups * rows * HEAD_DIM
        ),
    )(*arrays)


def unpack_kernel(per_group, source_ref, *refs):
    ins, out_ref = refs[:-1], refs[-1]
    rows = out_ref.shape[0]
    for k, src in enumerate(ins):
        for head in range(per_group):
            column = pl.multiple_of((source_ref[k] * per_group + head) * HEAD_DIM, HEAD_DIM)
            out_ref[:, pl.ds(column, HEAD_DIM)] = src[head * rows : (head + 1) * rows, :]


def unpack(source, parts, rows):
    vmem = pl.BlockSpec(memory_space=pltpu.VMEM)
    per_group = parts[0].shape[0] // rows
    columns = len(parts) * per_group * HEAD_DIM
    return pl.pallas_call(
        functools.partial(unpack_kernel, per_group),
        out_shape=jax.ShapeDtypeStruct((rows, columns), parts[0].dtype),
        in_specs=[pl.BlockSpec(memory_space=pltpu.SMEM)] + [vmem] * len(parts),
        out_specs=vmem,
        compiler_params=pltpu.CompilerParams(vmem_limit_bytes=VMEM_LIMIT),
        cost_estimate=pl.CostEstimate(flops=0, transcendentals=0, bytes_accessed=4 * rows * columns),
    )(source, *parts)


def dot(a, b, dims):
    return lax.dot_general(a, b, (dims, ((), ())), preferred_element_type=jnp.float32)


NN = ((1,), (0,))
NT = ((1,), (1,))


def head_kernel(kt, qt, nlow, nprior, ndq, count_ref, start_ref, target_ref, core_ref, source_ref, x_ref, *rest):
    low_refs, prior_refs, rest = rest[:nlow], rest[nlow : nlow + nprior], rest[nlow + nprior :]
    early_dq, rest = rest[:ndq], rest[ndq:]
    if nlow:
        keep_ref, give_ref, rest = rest[0], rest[1], rest[2:]
    else:
        d_ref, rest = rest[0], rest[1:]
    dq_refs, scratch = rest[:x_ref.shape[0]], rest[x_ref.shape[0]:]
    s_ref, p_ref, dq_ref = scratch[:3]
    if nlow:
        d_ref, full_ref, low_sem, prior_sem = scratch[3:7]
        bufs = scratch[7:]
        copies = gather_low(low_refs, full_ref, low_sem, source_ref)
        for n in range(nprior):
            copies.append(pltpu.make_async_copy(prior_refs[n], bufs[n], prior_sem.at[n]))
            copies[-1].start()
    groups = x_ref.shape[0]
    count = count_ref[0]
    start = start_ref[0]
    scale = HEAD_DIM ** (-0.5)
    factor = scale * math.log2(math.e)
    q = x_ref[:, 2 * kt : 2 * kt + qt, :].reshape(groups * qt, HEAD_DIM)
    g = x_ref[:, 2 * kt + qt : 2 * kt + 2 * qt, :].reshape(groups * qt, HEAD_DIM)
    q_pos = start + lax.broadcasted_iota(jnp.int32, g.shape, 0)
    g = jnp.where(q_pos < count, g.astype(jnp.float32), 0.0).astype(g.dtype)
    slab = q.shape[0]
    top = jnp.full((8, slab), -jnp.inf, jnp.float32)
    for c in range(groups):
        s = dot(x_ref[c, :kt, :], q, NT) * factor
        k_pos = c * kt + lax.broadcasted_iota(jnp.int32, s.shape, 0)
        s = jnp.where(k_pos < count, s, -1e30)
        s_ref[c] = s
        top = jnp.maximum(top, jnp.max(s.reshape(kt // 8, 8, slab), axis=0))
    top = jnp.max(top, axis=0, keepdims=True)
    total = jnp.zeros((8, slab), jnp.float32)
    row_dot = jnp.zeros((8, slab), jnp.float32)
    for c in range(groups):
        e = jnp.exp2(s_ref[c] - top)
        s_ref[c] = e
        gp = dot(x_ref[c, kt : 2 * kt, :], g, NT)
        p_ref[c] = gp
        total += jnp.sum(e.reshape(kt // 8, 8, slab), axis=0)
        row_dot += jnp.sum((e * gp).reshape(kt // 8, 8, slab), axis=0)
    inv = 1.0 / jnp.sum(total, axis=0, keepdims=True)
    row_dot = jnp.sum(row_dot, axis=0, keepdims=True) * inv
    dq_t = jnp.zeros((HEAD_DIM, slab), jnp.float32)
    for c in range(groups):
        w = s_ref[c] * inv
        ds = (w * (p_ref[c] - row_dot)).astype(jnp.bfloat16)
        rows = pl.ds(c * kt, kt)
        d_ref[rows, :HEAD_DIM] = (dot(ds, q, NN) * scale).astype(d_ref.dtype)
        d_ref[rows, HEAD_DIM:] = dot(w.astype(jnp.bfloat16), g, NN).astype(d_ref.dtype)
        dq_t += dot(x_ref[c, :kt, :].T, ds, NN)
    dq_ref[...] = (dq_t * scale).T.reshape(dq_ref.shape)
    for k in range(groups):
        row = 0
        for ref in early_dq[k::groups]:
            dq_refs[k][row : row + ref.shape[0], :] = ref[...]
            row += ref.shape[0]
        dq_refs[k][row : row + qt, :] = dq_ref[target_ref[k]].astype(dq_refs[k].dtype)
    if nlow:
        for copy in copies:
            copy.wait()
        results = []
        for ref in (*bufs, d_ref):
            for column in range(0, ref.shape[1], 2 * HEAD_DIM):
                part = ref[:, column : column + 2 * HEAD_DIM]
                results.append(spread(dot(full_ref[...], part, NN)))
        keep, give = divide(results, core_ref)
        keep_ref[...] = keep.astype(keep_ref.dtype)
        give_ref[...] = give.astype(give_ref.dtype)


def gather_low(low_refs, full_ref, sem, source_ref):
    ring = len(low_refs) // 2
    upper, near, far = low_refs[:ring], low_refs[ring : 2 * ring], low_refs[2 * ring]
    half, kt = near[0].shape
    copies = []

    def place(src, row, k):
        columns = pl.ds(pl.multiple_of(source_ref[k] * kt, kt), kt)
        copy = pltpu.make_async_copy(src, full_ref.at[pl.ds(row, half), columns], sem.at[len(copies)])
        copy.start()
        copies.append(copy)

    for k in range(ring):
        place(upper[k].at[0], 0, k)
        place(upper[k].at[1], 0, ring + k)
        place(near[k], half, k)
        place(far.at[k], half, ring + k)
    return copies


def divide(parts, core_ref):
    w = jnp.concatenate(parts, axis=2) if len(parts) > 1 else parts[0]
    w = w.reshape(DP_PAIRS, 2, -1, *w.shape[1:])
    even = core_ref[0] == 0
    return jnp.where(even, w[:, 0], w[:, 1]), jnp.where(even, w[:, 1], w[:, 0])


def spread(acc):
    tiles = acc.shape[0] // 8
    low_half = lax.broadcasted_iota(jnp.int32, (tiles, 8, HEAD_DIM), 1) < 4
    wk = acc[:, :HEAD_DIM].reshape(tiles, 8, HEAD_DIM)
    wv = acc[:, HEAD_DIM:].reshape(tiles, 8, HEAD_DIM)
    first = jnp.where(low_half, wk, pltpu.roll(wv, 4, 1))
    second = jnp.where(low_half, pltpu.roll(wk, 4, 1), wv)
    return jnp.stack([first, second], axis=1)


def head_grads(x, heads, scalars, kt, qt, rank, low=(), prior=(), early_dq=()):
    groups = x.shape[0]
    keys, slab, rows = groups * kt, groups * qt, 2 * kt + 2 * qt
    smem = pl.BlockSpec(memory_space=pltpu.SMEM)
    scratch = [
        pltpu.VMEM((groups, kt, slab), jnp.float32),
        pltpu.VMEM((groups, kt, slab), jnp.float32),
        pltpu.VMEM((groups, qt, HEAD_DIM), jnp.float32),
    ]
    if low:
        first = [split_shape(rank, 1 + sum(p.shape[1] for p in prior) // (2 * HEAD_DIM))] * 2
        first_spec = [pl.BlockSpec(e.shape, lambda n, rank=len(e.shape): (0,) * rank) for e in first]
        scratch += [
            pltpu.VMEM((keys, 2 * HEAD_DIM), jnp.bfloat16),
            pltpu.VMEM((rank, keys), jnp.bfloat16),
            pltpu.SemaphoreType.DMA((2 * groups,)),
            pltpu.SemaphoreType.DMA((len(prior),)),
        ] + [pltpu.VMEM(p.shape, p.dtype) for p in prior]
    else:
        first = [jax.ShapeDtypeStruct((keys, heads * 2 * HEAD_DIM), jnp.bfloat16)]
        first_spec = [pl.BlockSpec((keys, 2 * HEAD_DIM), lambda n: (0, n))]
    before = [p for parts in early_dq for p in parts]
    dq_rows = qt + sum(parts[0].shape[0] for parts in early_dq)
    out = pl.pallas_call(
        functools.partial(head_kernel, kt, qt, len(low), len(prior), len(before)),
        grid=(heads,),
        out_shape=first + [jax.ShapeDtypeStruct((heads * dq_rows, HEAD_DIM), jnp.bfloat16)] * groups,
        in_specs=[smem] * len(scalars)
        + [pl.BlockSpec((groups, rows, HEAD_DIM), lambda n: (0, n, 0))]
        + [pl.BlockSpec(memory_space=pl.ANY)] * (len(low) + len(prior))
        + [pl.BlockSpec(e.shape, lambda n, rank=e.ndim: (0,) * rank) for e in before],
        out_specs=first_spec + [pl.BlockSpec((dq_rows, HEAD_DIM), lambda n: (n, 0))] * groups,
        scratch_shapes=scratch,
        compiler_params=pltpu.CompilerParams(vmem_limit_bytes=VMEM_LIMIT),
        cost_estimate=pl.CostEstimate(
            flops=20 * heads * keys * slab * HEAD_DIM,
            transcendentals=heads * keys * slab,
            bytes_accessed=4 * x.size,
        ),
    )(*scalars, x, *low, *prior, *before)
    return out[: len(first)], out[len(first) :]


def split_shape(rank, heads):
    return jax.ShapeDtypeStruct((DP_PAIRS, rank // 16 // DP_PAIRS, 2, 8 * heads, HEAD_DIM), jnp.bfloat16)


def shifted(index, k, groups, sign):
    ring = groups // 2
    half, place = index // ring, index % ring
    return (half + k // ring) % 2 * ring + (place + sign * (k % ring) + ring) % ring


def body(queries, keys, values, out_grad, layer_input, projection, token_counts, slab_start):
    groups = lax.axis_size("seq")
    clips = lax.axis_size("dp")
    kt, qt = keys.shape[1], queries.shape[1]
    heads = keys.shape[2] // HEAD_DIM // groups
    me = lax.axis_index("seq")
    ways = jnp.arange(groups, dtype=jnp.int32)
    target = shifted(me, ways, groups, 1)
    source = shifted(me, ways, groups, -1)

    def send(x, k):
        return lax.ppermute(x, "seq", [(i, shifted(i, k, groups, 1)) for i in range(groups)])

    def exchange(x):
        return lax.all_to_all(x, "seq", split_axis=0, concat_axis=0, tiled=True)

    def after(x, *others):
        return lax.optimization_barrier((x, *others))

    clip = lax.axis_index("dp")
    scalars = (token_counts, slab_start, target, (clip % 2).reshape(1), source)

    rank = projection.shape[1]

    def attend(part, count, *more):
        return head_grads(part, count, scalars, kt, qt, rank, *more)

    def other_core(x):
        return lax.ppermute(x, "dp", [(i, i ^ 1) for i in range(clips)])

    first, second = tuple(range(heads - 1)), (heads - 1,)
    arrays = (keys[0], values[0], queries[0], out_grad[0])
    part0, = pack(arrays, (first,), groups)
    rest, part0 = after((arrays, layer_input), part0)
    arrays, layer_input = rest
    got0 = exchange(part0)
    low = jnp.dot(layer_input[0], projection, preferred_element_type=jnp.float32).astype(jnp.bfloat16).T
    part1, = pack(arrays, (second,), groups)
    ring = groups // 2
    upper, lower = low[: rank // 2], low[rank // 2 :]
    upper = jnp.stack([upper, send(upper, ring)])
    near = [lower] + [send(lower, k) for k in range(1, ring)]
    part1, got0, upper, near = after(part1, got0, upper, near)
    got1 = exchange(part1)
    low = [upper] + [send(upper, k) for k in range(1, ring)] + near + [send(jnp.stack(near), ring)]
    d0, dq0 = attend(got0, len(first))
    (keep, give), dq = attend(got1, len(second), low, d0, [dq0])

    back = [dq[0]] + [send(dq[k], k) for k in range(1, groups)]
    query_grad = unpack(source, back, qt)[None]
    mine = (keep.astype(jnp.float32) + other_core(give).astype(jnp.float32)).astype(jnp.bfloat16)
    mine = mine.reshape(-1, heads * 8, HEAD_DIM)
    alike = [
        [i * groups + j for i in range(core, clips, 2) for j in range(groups)] for core in range(2)
    ]
    got = lax.all_to_all(
        mine, ("dp", "seq"), split_axis=0, concat_axis=0, axis_index_groups=alike, tiled=True
    )
    got = got.reshape(clips // 2, groups, heads, 2, 4, HEAD_DIM).astype(jnp.float32)
    total = jnp.sum(got, axis=0) * (1.0 / clips)
    projected = jnp.transpose(total, (3, 2, 0, 1, 4)).reshape(4, 2, groups * heads * HEAD_DIM)
    return (query_grad, projected)


def solution(mesh):
    return jax.shard_map(
        body,
        mesh=mesh,
        in_specs=(
            P("dp", "seq", None),
            P("dp", "seq", None),
            P("dp", "seq", None),
            P("dp", "seq", None),
            P("dp", "seq", None),
            P(),
            P("dp"),
            P("dp"),
        ),
        out_specs=(P("dp", "seq", None), P(("dp", "seq"), None, None)),
        check_vma=False,
    )
```

```python
import functools
import math

import jax
import jax.numpy as jnp
from jax import lax
from jax.experimental import pallas as pl
from jax.experimental.pallas import tpu as pltpu
from jax.sharding import PartitionSpec as P

HEAD_DIM = 128
VMEM_LIMIT = 60 * 1024 * 1024
UNPACK_VMEM = 8 * 1024 * 1024
DP_PAIRS = 8


def pack_kernel(pieces, groups, *refs):
    sources, refs = refs[:4], refs[4:]
    n = len(pieces)
    outs, bufs, in_sem, out_sem = refs[:n], refs[n : 2 * n], refs[2 * n], refs[2 * n + 1]
    per_group = sources[0].shape[1] // HEAD_DIM // groups
    loads, stores = {}, []
    count = 0
    for p, heads in enumerate(pieces):
        for j in range(groups):
            row = 0
            loads[p, j] = []
            for head in heads:
                for src in sources:
                    rows = src.shape[0]
                    columns = pl.ds((j * per_group + head) * HEAD_DIM, HEAD_DIM)
                    copy = pltpu.make_async_copy(
                        src.at[:, columns], bufs[p].at[j, pl.ds(row, rows), :], in_sem.at[count]
                    )
                    copy.start()
                    loads[p, j].append(copy)
                    count += 1
                    row += rows
    for p in range(n):
        for j in range(groups):
            for copy in loads[p, j]:
                copy.wait()
            copy = pltpu.make_async_copy(bufs[p].at[j], outs[p].at[j], out_sem.at[len(stores)])
            copy.start()
            stores.append(copy)
    for copy in stores:
        copy.wait()


def pack(arrays, pieces, groups):
    rows = sum(x.shape[0] for x in arrays)
    heads = sum(len(p) for p in pieces)
    hbm = pl.BlockSpec(memory_space=pl.ANY)
    shapes = [(groups, len(p) * rows, HEAD_DIM) for p in pieces]
    return pl.pallas_call(
        functools.partial(pack_kernel, pieces, groups),
        out_shape=[jax.ShapeDtypeStruct(e, arrays[0].dtype) for e in shapes],
        in_specs=[hbm] * len(arrays),
        out_specs=[hbm] * len(pieces),
        scratch_shapes=[pltpu.VMEM(e, arrays[0].dtype) for e in shapes]
        + [
            pltpu.SemaphoreType.DMA((len(arrays) * groups * heads,)),
            pltpu.SemaphoreType.DMA((groups * len(pieces),)),
        ],
        compiler_params=pltpu.CompilerParams(vmem_limit_bytes=VMEM_LIMIT),
        cost_estimate=pl.CostEstimate(
            flops=0, transcendentals=0, bytes_accessed=4 * heads * groups * rows * HEAD_DIM
        ),
    )(*arrays)


def unpack_kernel(per_group, source_ref, *refs):
    ins, out_ref = refs[:-1], refs[-1]
    rows = out_ref.shape[0]
    for k, src in enumerate(ins):
        for head in range(per_group):
            column = pl.multiple_of((source_ref[k] * per_group + head) * HEAD_DIM, HEAD_DIM)
            out_ref[:, pl.ds(column, HEAD_DIM)] = src[head * rows : (head + 1) * rows, :]


def unpack(source, parts, rows):
    vmem = pl.BlockSpec(memory_space=pltpu.VMEM)
    per_group = parts[0].shape[0] // rows
    columns = len(parts) * per_group * HEAD_DIM
    return pl.pallas_call(
        functools.partial(unpack_kernel, per_group),
        out_shape=jax.ShapeDtypeStruct((rows, columns), parts[0].dtype),
        in_specs=[pl.BlockSpec(memory_space=pltpu.SMEM)] + [vmem] * len(parts),
        out_specs=vmem,
        compiler_params=pltpu.CompilerParams(vmem_limit_bytes=UNPACK_VMEM),
        cost_estimate=pl.CostEstimate(flops=0, transcendentals=0, bytes_accessed=4 * rows * columns),
    )(source, *parts)


def dot(a, b, dims):
    return lax.dot_general(a, b, (dims, ((), ())), preferred_element_type=jnp.float32)


NN = ((1,), (0,))
NT = ((1,), (1,))


def head_kernel(kt, qt, nlow, nprior, ndq, count_ref, start_ref, target_ref, core_ref, source_ref, x_ref, *rest):
    low_refs, prior_refs, rest = rest[:nlow], rest[nlow : nlow + nprior], rest[nlow + nprior :]
    early_dq, rest = rest[:ndq], rest[ndq:]
    if nlow:
        keep_ref, give_ref, rest = rest[0], rest[1], rest[2:]
    else:
        d_ref, rest = rest[0], rest[1:]
    dq_refs, scratch = rest[:x_ref.shape[0]], rest[x_ref.shape[0]:]
    s_ref, p_ref, dq_ref = scratch[:3]
    if nlow:
        d_ref, full_ref, low_sem, prior_sem = scratch[3:7]
        bufs = scratch[7:]
        copies = gather_low(low_refs, full_ref, low_sem, source_ref)
        for n in range(nprior):
            copies.append(pltpu.make_async_copy(prior_refs[n], bufs[n], prior_sem.at[n]))
            copies[-1].start()
    groups = x_ref.shape[0]
    count = count_ref[0]
    start = start_ref[0]
    scale = HEAD_DIM ** (-0.5)
    factor = scale * math.log2(math.e)
    q = x_ref[:, 2 * kt : 2 * kt + qt, :].reshape(groups * qt, HEAD_DIM)
    g = x_ref[:, 2 * kt + qt : 2 * kt + 2 * qt, :].reshape(groups * qt, HEAD_DIM)
    q_pos = start + lax.broadcasted_iota(jnp.int32, g.shape, 0)
    g = jnp.where(q_pos < count, g.astype(jnp.float32), 0.0).astype(g.dtype)
    slab = q.shape[0]
    top = jnp.full((8, slab), -jnp.inf, jnp.float32)
    for c in range(groups):
        s = dot(x_ref[c, :kt, :], q, NT) * factor
        k_pos = c * kt + lax.broadcasted_iota(jnp.int32, s.shape, 0)
        s = jnp.where(k_pos < count, s, -1e30)
        s_ref[c] = s
        top = jnp.maximum(top, jnp.max(s.reshape(kt // 8, 8, slab), axis=0))
    top = jnp.max(top, axis=0, keepdims=True)
    total = jnp.zeros((8, slab), jnp.float32)
    row_dot = jnp.zeros((8, slab), jnp.float32)
    for c in range(groups):
        e = jnp.exp2(s_ref[c] - top)
        s_ref[c] = e
        gp = dot(x_ref[c, kt : 2 * kt, :], g, NT)
        p_ref[c] = gp
        total += jnp.sum(e.reshape(kt // 8, 8, slab), axis=0)
        row_dot += jnp.sum((e * gp).reshape(kt // 8, 8, slab), axis=0)
    inv = 1.0 / jnp.sum(total, axis=0, keepdims=True)
    row_dot = jnp.sum(row_dot, axis=0, keepdims=True) * inv
    dq_t = jnp.zeros((HEAD_DIM, slab), jnp.float32)
    for c in range(groups):
        w = s_ref[c] * inv
        ds = (w * (p_ref[c] - row_dot)).astype(jnp.bfloat16)
        rows = pl.ds(c * kt, kt)
        d_ref[rows, :HEAD_DIM] = (dot(ds, q, NN) * scale).astype(d_ref.dtype)
        d_ref[rows, HEAD_DIM:] = dot(w.astype(jnp.bfloat16), g, NN).astype(d_ref.dtype)
        dq_t += dot(x_ref[c, :kt, :].T, ds, NN)
    dq_ref[...] = (dq_t * scale).T.reshape(dq_ref.shape)
    for k in range(groups):
        row = 0
        for ref in early_dq[k::groups]:
            dq_refs[k][row : row + ref.shape[0], :] = ref[...]
            row += ref.shape[0]
        dq_refs[k][row : row + qt, :] = dq_ref[target_ref[k]].astype(dq_refs[k].dtype)
    if nlow:
        for copy in copies:
            copy.wait()
        results = []
        for ref in (*bufs, d_ref):
            for column in range(0, ref.shape[1], 2 * HEAD_DIM):
                part = ref[:, column : column + 2 * HEAD_DIM]
                results.append(spread(dot(full_ref[...], part, NN)))
        keep, give = divide(results, core_ref)
        keep_ref[...] = keep.astype(keep_ref.dtype)
        give_ref[...] = give.astype(give_ref.dtype)


def gather_low(low_refs, full_ref, sem, source_ref):
    ring = len(low_refs) // 2
    upper, near, far = low_refs[:ring], low_refs[ring : 2 * ring], low_refs[2 * ring]
    half, kt = near[0].shape
    copies = []

    def place(src, row, k):
        columns = pl.ds(pl.multiple_of(source_ref[k] * kt, kt), kt)
        copy = pltpu.make_async_copy(src, full_ref.at[pl.ds(row, half), columns], sem.at[len(copies)])
        copy.start()
        copies.append(copy)

    for k in range(ring):
        place(upper[k].at[0], 0, k)
        place(upper[k].at[1], 0, ring + k)
        place(near[k], half, k)
        place(far.at[k], half, ring + k)
    return copies


def divide(parts, core_ref):
    w = jnp.concatenate(parts, axis=2) if len(parts) > 1 else parts[0]
    w = w.reshape(DP_PAIRS, 2, -1, *w.shape[1:])
    even = core_ref[0] == 0
    return jnp.where(even, w[:, 0], w[:, 1]), jnp.where(even, w[:, 1], w[:, 0])


def spread(acc):
    tiles = acc.shape[0] // 8
    low_half = lax.broadcasted_iota(jnp.int32, (tiles, 8, HEAD_DIM), 1) < 4
    wk = acc[:, :HEAD_DIM].reshape(tiles, 8, HEAD_DIM)
    wv = acc[:, HEAD_DIM:].reshape(tiles, 8, HEAD_DIM)
    first = jnp.where(low_half, wk, pltpu.roll(wv, 4, 1))
    second = jnp.where(low_half, pltpu.roll(wk, 4, 1), wv)
    return jnp.stack([first, second], axis=1)


def head_grads(x, heads, scalars, kt, qt, rank, low=(), prior=(), early_dq=()):
    groups = x.shape[0]
    keys, slab, rows = groups * kt, groups * qt, 2 * kt + 2 * qt
    smem = pl.BlockSpec(memory_space=pltpu.SMEM)
    scratch = [
        pltpu.VMEM((groups, kt, slab), jnp.float32),
        pltpu.VMEM((groups, kt, slab), jnp.float32),
        pltpu.VMEM((groups, qt, HEAD_DIM), jnp.float32),
    ]
    if low:
        first = [split_shape(rank, 1 + sum(p.shape[1] for p in prior) // (2 * HEAD_DIM))] * 2
        first_spec = [pl.BlockSpec(e.shape, lambda n, rank=len(e.shape): (0,) * rank) for e in first]
        scratch += [
            pltpu.VMEM((keys, 2 * HEAD_DIM), jnp.bfloat16),
            pltpu.VMEM((rank, keys), jnp.bfloat16),
            pltpu.SemaphoreType.DMA((2 * groups,)),
            pltpu.SemaphoreType.DMA((len(prior),)),
        ] + [pltpu.VMEM(p.shape, p.dtype) for p in prior]
    else:
        first = [jax.ShapeDtypeStruct((keys, heads * 2 * HEAD_DIM), jnp.bfloat16)]
        first_spec = [pl.BlockSpec((keys, 2 * HEAD_DIM), lambda n: (0, n))]
    before = [p for parts in early_dq for p in parts]
    dq_rows = qt + sum(parts[0].shape[0] for parts in early_dq)
    out = pl.pallas_call(
        functools.partial(head_kernel, kt, qt, len(low), len(prior), len(before)),
        grid=(heads,),
        out_shape=first + [jax.ShapeDtypeStruct((heads * dq_rows, HEAD_DIM), jnp.bfloat16)] * groups,
        in_specs=[smem] * len(scalars)
        + [pl.BlockSpec((groups, rows, HEAD_DIM), lambda n: (0, n, 0))]
        + [pl.BlockSpec(memory_space=pl.ANY)] * (len(low) + len(prior))
        + [pl.BlockSpec(e.shape, lambda n, rank=e.ndim: (0,) * rank) for e in before],
        out_specs=first_spec + [pl.BlockSpec((dq_rows, HEAD_DIM), lambda n: (n, 0))] * groups,
        scratch_shapes=scratch,
        compiler_params=pltpu.CompilerParams(vmem_limit_bytes=VMEM_LIMIT),
        cost_estimate=pl.CostEstimate(
            flops=20 * heads * keys * slab * HEAD_DIM,
            transcendentals=heads * keys * slab,
            bytes_accessed=4 * x.size,
        ),
    )(*scalars, x, *low, *prior, *before)
    return out[: len(first)], out[len(first) :]


def split_shape(rank, heads):
    return jax.ShapeDtypeStruct((DP_PAIRS, rank // 16 // DP_PAIRS, 2, 8 * heads, HEAD_DIM), jnp.bfloat16)


def shifted(index, k, groups, sign):
    ring = groups // 2
    half, place = index // ring, index % ring
    return (half + k // ring) % 2 * ring + (place + sign * (k % ring) + ring) % ring


def body(queries, keys, values, out_grad, layer_input, projection, token_counts, slab_start):
    groups = lax.axis_size("seq")
    clips = lax.axis_size("dp")
    kt, qt = keys.shape[1], queries.shape[1]
    heads = keys.shape[2] // HEAD_DIM // groups
    me = lax.axis_index("seq")
    ways = jnp.arange(groups, dtype=jnp.int32)
    target = shifted(me, ways, groups, 1)
    source = shifted(me, ways, groups, -1)

    def send(x, k):
        return lax.ppermute(x, "seq", [(i, shifted(i, k, groups, 1)) for i in range(groups)])

    def exchange(x):
        return lax.all_to_all(x, "seq", split_axis=0, concat_axis=0, tiled=True)

    def after(x, *others):
        return lax.optimization_barrier((x, *others))

    clip = lax.axis_index("dp")
    scalars = (token_counts, slab_start, target, (clip % 2).reshape(1), source)

    rank = projection.shape[1]

    def attend(part, count, *more):
        return head_grads(part, count, scalars, kt, qt, rank, *more)

    def other_core(x):
        return lax.ppermute(x, "dp", [(i, i ^ 1) for i in range(clips)])

    first, second = tuple(range(heads - 1)), (heads - 1,)
    arrays = (keys[0], values[0], queries[0], out_grad[0])
    part0, = pack(arrays, (first,), groups)
    rest, part0 = after((arrays, layer_input), part0)
    arrays, layer_input = rest
    got0 = exchange(part0)
    low = jnp.dot(layer_input[0], projection, preferred_element_type=jnp.float32).astype(jnp.bfloat16).T
    part1, = pack(arrays, (second,), groups)
    ring = groups // 2
    upper, lower = low[: rank // 2], low[rank // 2 :]
    upper = jnp.stack([upper, send(upper, ring)])
    near = [lower] + [send(lower, k) for k in range(1, ring)]
    part1, got0, upper, near = after(part1, got0, upper, near)
    got1 = exchange(part1)
    low = [upper] + [send(upper, k) for k in range(1, ring)] + near + [send(jnp.stack(near), ring)]
    d0, dq0 = attend(got0, len(first))
    (keep, give), dq = attend(got1, len(second), low, d0, [dq0])

    back = [dq[0]] + [send(dq[k], k) for k in range(1, groups)]
    query_grad = unpack(source, back, qt)[None]
    mine = (keep.astype(jnp.float32) + other_core(give).astype(jnp.float32)).astype(jnp.bfloat16)
    mine = mine.reshape(-1, heads * 8, HEAD_DIM)
    alike = [
        [i * groups + j for i in range(core, clips, 2) for j in range(groups)] for core in range(2)
    ]
    got = lax.all_to_all(
        mine, ("dp", "seq"), split_axis=0, concat_axis=0, axis_index_groups=alike, tiled=True
    )
    got = got.reshape(clips // 2, groups, heads, 2, 4, HEAD_DIM).astype(jnp.float32)
    total = jnp.sum(got, axis=0) * (1.0 / clips)
    projected = jnp.transpose(total, (3, 2, 0, 1, 4)).reshape(4, 2, groups * heads * HEAD_DIM)
    return (query_grad, projected)


def solution(mesh):
    return jax.shard_map(
        body,
        mesh=mesh,
        in_specs=(
            P("dp", "seq", None),
            P("dp", "seq", None),
            P("dp", "seq", None),
            P("dp", "seq", None),
            P("dp", "seq", None),
            P(),
            P("dp"),
            P("dp"),
        ),
        out_specs=(P("dp", "seq", None), P(("dp", "seq"), None, None)),
        check_vma=False,
    )
```

```python
import functools
import math

import jax
import jax.numpy as jnp
from jax import lax
from jax.experimental import pallas as pl
from jax.experimental.pallas import tpu as pltpu
from jax.sharding import PartitionSpec as P

HEAD_DIM = 128
VMEM_LIMIT = 60 * 1024 * 1024
UNPACK_VMEM = 8 * 1024 * 1024
DP_PAIRS = 8


def pack_kernel(pieces, groups, *refs):
    sources, refs = refs[:4], refs[4:]
    n = len(pieces)
    outs, bufs, in_sem, out_sem = refs[:n], refs[n : 2 * n], refs[2 * n], refs[2 * n + 1]
    per_group = sources[0].shape[1] // HEAD_DIM // groups
    loads, stores = {}, []
    count = 0
    for p, heads in enumerate(pieces):
        for j in range(groups):
            row = 0
            loads[p, j] = []
            for head in heads:
                for src in sources:
                    rows = src.shape[0]
                    columns = pl.ds((j * per_group + head) * HEAD_DIM, HEAD_DIM)
                    copy = pltpu.make_async_copy(
                        src.at[:, columns], bufs[p].at[j, pl.ds(row, rows), :], in_sem.at[count]
                    )
                    copy.start()
                    loads[p, j].append(copy)
                    count += 1
                    row += rows
    for p in range(n):
        for j in range(groups):
            for copy in loads[p, j]:
                copy.wait()
            copy = pltpu.make_async_copy(bufs[p].at[j], outs[p].at[j], out_sem.at[len(stores)])
            copy.start()
            stores.append(copy)
    for copy in stores:
        copy.wait()


def pack(arrays, pieces, groups):
    rows = sum(x.shape[0] for x in arrays)
    heads = sum(len(p) for p in pieces)
    hbm = pl.BlockSpec(memory_space=pl.ANY)
    shapes = [(groups, len(p) * rows, HEAD_DIM) for p in pieces]
    return pl.pallas_call(
        functools.partial(pack_kernel, pieces, groups),
        out_shape=[jax.ShapeDtypeStruct(e, arrays[0].dtype) for e in shapes],
        in_specs=[hbm] * len(arrays),
        out_specs=[hbm] * len(pieces),
        scratch_shapes=[pltpu.VMEM(e, arrays[0].dtype) for e in shapes]
        + [
            pltpu.SemaphoreType.DMA((len(arrays) * groups * heads,)),
            pltpu.SemaphoreType.DMA((groups * len(pieces),)),
        ],
        compiler_params=pltpu.CompilerParams(vmem_limit_bytes=VMEM_LIMIT),
        cost_estimate=pl.CostEstimate(
            flops=0, transcendentals=0, bytes_accessed=4 * heads * groups * rows * HEAD_DIM
        ),
    )(*arrays)


def unpack_kernel(per_group, source_ref, *refs):
    ins, out_ref = refs[:-1], refs[-1]
    rows = out_ref.shape[0]
    for k, src in enumerate(ins):
        for head in range(per_group):
            column = pl.multiple_of((source_ref[k] * per_group + head) * HEAD_DIM, HEAD_DIM)
            out_ref[:, pl.ds(column, HEAD_DIM)] = src[head * rows : (head + 1) * rows, :]


def unpack(source, parts, rows):
    vmem = pl.BlockSpec(memory_space=pltpu.VMEM)
    per_group = parts[0].shape[0] // rows
    columns = len(parts) * per_group * HEAD_DIM
    return pl.pallas_call(
        functools.partial(unpack_kernel, per_group),
        out_shape=jax.ShapeDtypeStruct((rows, columns), parts[0].dtype),
        in_specs=[pl.BlockSpec(memory_space=pltpu.SMEM)] + [vmem] * len(parts),
        out_specs=vmem,
        compiler_params=pltpu.CompilerParams(vmem_limit_bytes=UNPACK_VMEM),
        cost_estimate=pl.CostEstimate(flops=0, transcendentals=0, bytes_accessed=4 * rows * columns),
    )(source, *parts)


def dot(a, b, dims):
    return lax.dot_general(a, b, (dims, ((), ())), preferred_element_type=jnp.float32)


NN = ((1,), (0,))
NT = ((1,), (1,))


def head_kernel(kt, qt, nlow, nprior, ndq, count_ref, start_ref, target_ref, core_ref, source_ref, x_ref, *rest):
    low_refs, prior_refs, rest = rest[:nlow], rest[nlow : nlow + nprior], rest[nlow + nprior :]
    early_dq, rest = rest[:ndq], rest[ndq:]
    if nlow:
        keep_ref, give_ref, rest = rest[0], rest[1], rest[2:]
    else:
        d_ref, rest = rest[0], rest[1:]
    dq_refs, scratch = rest[:x_ref.shape[0]], rest[x_ref.shape[0]:]
    s_ref, p_ref, dq_ref = scratch[:3]
    if nlow:
        d_ref, full_ref, low_sem, prior_sem = scratch[3:7]
        bufs = scratch[7:]
        copies = gather_low(low_refs, full_ref, low_sem, source_ref)
        for n in range(nprior):
            copies.append(pltpu.make_async_copy(prior_refs[n], bufs[n], prior_sem.at[n]))
            copies[-1].start()
    groups = x_ref.shape[0]
    count = count_ref[0]
    start = start_ref[0]
    scale = HEAD_DIM ** (-0.5)
    factor = scale * math.log2(math.e)
    q = x_ref[:, 2 * kt : 2 * kt + qt, :].reshape(groups * qt, HEAD_DIM)
    g = x_ref[:, 2 * kt + qt : 2 * kt + 2 * qt, :].reshape(groups * qt, HEAD_DIM)
    q_pos = start + lax.broadcasted_iota(jnp.int32, g.shape, 0)
    g = jnp.where(q_pos < count, g.astype(jnp.float32), 0.0).astype(g.dtype)
    slab = q.shape[0]
    top = jnp.full((8, slab), -jnp.inf, jnp.float32)
    for c in range(groups):
        s = dot(x_ref[c, :kt, :], q, NT) * factor
        k_pos = c * kt + lax.broadcasted_iota(jnp.int32, s.shape, 0)
        s = jnp.where(k_pos < count, s, -1e30)
        s_ref[c] = s
        top = jnp.maximum(top, jnp.max(s.reshape(kt // 8, 8, slab), axis=0))
    top = jnp.max(top, axis=0, keepdims=True)
    total = jnp.zeros((8, slab), jnp.float32)
    row_dot = jnp.zeros((8, slab), jnp.float32)
    for c in range(groups):
        e = jnp.exp2(s_ref[c] - top)
        s_ref[c] = e
        gp = dot(x_ref[c, kt : 2 * kt, :], g, NT)
        p_ref[c] = gp
        total += jnp.sum(e.reshape(kt // 8, 8, slab), axis=0)
        row_dot += jnp.sum((e * gp).reshape(kt // 8, 8, slab), axis=0)
    inv = 1.0 / jnp.sum(total, axis=0, keepdims=True)
    row_dot = jnp.sum(row_dot, axis=0, keepdims=True) * inv
    dq_t = jnp.zeros((HEAD_DIM, slab), jnp.float32)
    for c in range(groups):
        w = s_ref[c] * inv
        ds = (w * (p_ref[c] - row_dot)).astype(jnp.bfloat16)
        rows = pl.ds(c * kt, kt)
        d_ref[rows, :HEAD_DIM] = (dot(ds, q, NN) * scale).astype(d_ref.dtype)
        d_ref[rows, HEAD_DIM:] = dot(w.astype(jnp.bfloat16), g, NN).astype(d_ref.dtype)
        dq_t += dot(x_ref[c, :kt, :].T, ds, NN)
    dq_ref[...] = (dq_t * scale).T.reshape(dq_ref.shape)
    for k in range(groups):
        row = 0
        for ref in early_dq[k::groups]:
            dq_refs[k][row : row + ref.shape[0], :] = ref[...]
            row += ref.shape[0]
        dq_refs[k][row : row + qt, :] = dq_ref[target_ref[k]].astype(dq_refs[k].dtype)
    if nlow:
        for copy in copies:
            copy.wait()
        results = []
        for ref in (*bufs, d_ref):
            for column in range(0, ref.shape[1], 2 * HEAD_DIM):
                part = ref[:, column : column + 2 * HEAD_DIM]
                results.append(spread(dot(full_ref[...], part, NN)))
        keep, give = divide(results, core_ref)
        keep_ref[...] = keep.astype(keep_ref.dtype)
        give_ref[...] = give.astype(give_ref.dtype)


def gather_low(low_refs, full_ref, sem, source_ref):
    ring = len(low_refs) // 2
    upper, near, far = low_refs[:ring], low_refs[ring : 2 * ring], low_refs[2 * ring]
    half, kt = near[0].shape
    copies = []

    def place(src, row, k):
        columns = pl.ds(pl.multiple_of(source_ref[k] * kt, kt), kt)
        copy = pltpu.make_async_copy(src, full_ref.at[pl.ds(row, half), columns], sem.at[len(copies)])
        copy.start()
        copies.append(copy)

    for k in range(ring):
        place(upper[k].at[0], 0, k)
        place(upper[k].at[1], 0, ring + k)
        place(near[k], half, k)
        place(far.at[k], half, ring + k)
    return copies


def divide(parts, core_ref):
    w = jnp.concatenate(parts, axis=2) if len(parts) > 1 else parts[0]
    w = w.reshape(DP_PAIRS, 2, -1, *w.shape[1:])
    even = core_ref[0] == 0
    return jnp.where(even, w[:, 0], w[:, 1]), jnp.where(even, w[:, 1], w[:, 0])


def spread(acc):
    tiles = acc.shape[0] // 8
    low_half = lax.broadcasted_iota(jnp.int32, (tiles, 8, HEAD_DIM), 1) < 4
    wk = acc[:, :HEAD_DIM].reshape(tiles, 8, HEAD_DIM)
    wv = acc[:, HEAD_DIM:].reshape(tiles, 8, HEAD_DIM)
    first = jnp.where(low_half, wk, pltpu.roll(wv, 4, 1))
    second = jnp.where(low_half, pltpu.roll(wk, 4, 1), wv)
    return jnp.stack([first, second], axis=1)


def head_grads(x, heads, scalars, kt, qt, rank, low=(), prior=(), early_dq=()):
    groups = x.shape[0]
    keys, slab, rows = groups * kt, groups * qt, 2 * kt + 2 * qt
    smem = pl.BlockSpec(memory_space=pltpu.SMEM)
    scratch = [
        pltpu.VMEM((groups, kt, slab), jnp.float32),
        pltpu.VMEM((groups, kt, slab), jnp.float32),
        pltpu.VMEM((groups, qt, HEAD_DIM), jnp.float32),
    ]
    if low:
        first = [split_shape(rank, 1 + sum(p.shape[1] for p in prior) // (2 * HEAD_DIM))] * 2
        first_spec = [pl.BlockSpec(e.shape, lambda n, rank=len(e.shape): (0,) * rank) for e in first]
        scratch += [
            pltpu.VMEM((keys, 2 * HEAD_DIM), jnp.bfloat16),
            pltpu.VMEM((rank, keys), jnp.bfloat16),
            pltpu.SemaphoreType.DMA((2 * groups,)),
            pltpu.SemaphoreType.DMA((len(prior),)),
        ] + [pltpu.VMEM(p.shape, p.dtype) for p in prior]
    else:
        first = [jax.ShapeDtypeStruct((keys, heads * 2 * HEAD_DIM), jnp.bfloat16)]
        first_spec = [pl.BlockSpec((keys, 2 * HEAD_DIM), lambda n: (0, n))]
    before = [p for parts in early_dq for p in parts]
    dq_rows = qt + sum(parts[0].shape[0] for parts in early_dq)
    out = pl.pallas_call(
        functools.partial(head_kernel, kt, qt, len(low), len(prior), len(before)),
        grid=(heads,),
        out_shape=first + [jax.ShapeDtypeStruct((heads * dq_rows, HEAD_DIM), jnp.bfloat16)] * groups,
        in_specs=[smem] * len(scalars)
        + [pl.BlockSpec((groups, rows, HEAD_DIM), lambda n: (0, n, 0))]
        + [pl.BlockSpec(memory_space=pl.ANY)] * (len(low) + len(prior))
        + [pl.BlockSpec(e.shape, lambda n, rank=e.ndim: (0,) * rank) for e in before],
        out_specs=first_spec + [pl.BlockSpec((dq_rows, HEAD_DIM), lambda n: (n, 0))] * groups,
        scratch_shapes=scratch,
        compiler_params=pltpu.CompilerParams(vmem_limit_bytes=VMEM_LIMIT),
        cost_estimate=pl.CostEstimate(
            flops=20 * heads * keys * slab * HEAD_DIM,
            transcendentals=heads * keys * slab,
            bytes_accessed=4 * x.size,
        ),
    )(*scalars, x, *low, *prior, *before)
    return out[: len(first)], out[len(first) :]


def split_shape(rank, heads):
    return jax.ShapeDtypeStruct((DP_PAIRS, rank // 16 // DP_PAIRS, 2, 8 * heads, HEAD_DIM), jnp.bfloat16)


def shifted(index, k, groups, sign):
    ring = groups // 2
    half, place = index // ring, index % ring
    return (half + k // ring) % 2 * ring + (place + sign * (k % ring) + ring) % ring


def body(queries, keys, values, out_grad, layer_input, projection, token_counts, slab_start):
    groups = lax.axis_size("seq")
    clips = lax.axis_size("dp")
    kt, qt = keys.shape[1], queries.shape[1]
    heads = keys.shape[2] // HEAD_DIM // groups
    me = lax.axis_index("seq")
    ways = jnp.arange(groups, dtype=jnp.int32)
    target = shifted(me, ways, groups, 1)
    source = shifted(me, ways, groups, -1)

    def send(x, k):
        return lax.ppermute(x, "seq", [(i, shifted(i, k, groups, 1)) for i in range(groups)])

    def exchange(x):
        return lax.all_to_all(x, "seq", split_axis=0, concat_axis=0, tiled=True)

    def after(x, *others):
        return lax.optimization_barrier((x, *others))

    clip = lax.axis_index("dp")
    scalars = (token_counts, slab_start, target, (clip % 2).reshape(1), source)

    rank = projection.shape[1]

    def attend(part, count, *more):
        return head_grads(part, count, scalars, kt, qt, rank, *more)

    def other_core(x):
        return lax.ppermute(x, "dp", [(i, i ^ 1) for i in range(clips)])

    first, second = tuple(range(heads - 1)), (heads - 1,)
    arrays = (keys[0], values[0], queries[0], out_grad[0])
    part0, = pack(arrays, (first,), groups)
    rest, part0 = after((arrays, layer_input), part0)
    arrays, layer_input = rest
    got0 = exchange(part0)
    low = jnp.dot(layer_input[0], projection, preferred_element_type=jnp.float32).astype(jnp.bfloat16).T
    part1, = pack(arrays, (second,), groups)
    ring = groups // 2
    upper, lower = low[: rank // 2], low[rank // 2 :]
    upper = jnp.stack([upper, send(upper, ring)])
    near = [lower] + [send(lower, k) for k in range(1, ring)]
    part1, got0 = after(part1, got0)
    got1 = exchange(part1)
    low = [upper] + [send(upper, k) for k in range(1, ring)] + near + [send(jnp.stack(near), ring)]
    d0, dq0 = attend(got0, len(first))
    (keep, give), dq = attend(got1, len(second), low, d0, [dq0])

    back = [dq[0]] + [send(dq[k], k) for k in range(1, groups)]
    query_grad = unpack(source, back, qt)[None]
    mine = (keep.astype(jnp.float32) + other_core(give).astype(jnp.float32)).astype(jnp.bfloat16)
    mine = mine.reshape(-1, heads * 8, HEAD_DIM)
    alike = [
        [i * groups + j for i in range(core, clips, 2) for j in range(groups)] for core in range(2)
    ]
    got = lax.all_to_all(
        mine, ("dp", "seq"), split_axis=0, concat_axis=0, axis_index_groups=alike, tiled=True
    )
    got = got.reshape(clips // 2, groups, heads, 2, 4, HEAD_DIM).astype(jnp.float32)
    total = jnp.sum(got, axis=0) * (1.0 / clips)
    projected = jnp.transpose(total, (3, 2, 0, 1, 4)).reshape(4, 2, groups * heads * HEAD_DIM)
    return (query_grad, projected)


def solution(mesh):
    return jax.shard_map(
        body,
        mesh=mesh,
        in_specs=(
            P("dp", "seq", None),
            P("dp", "seq", None),
            P("dp", "seq", None),
            P("dp", "seq", None),
            P("dp", "seq", None),
            P(),
            P("dp"),
            P("dp"),
        ),
        out_specs=(P("dp", "seq", None), P(("dp", "seq"), None, None)),
        check_vma=False,
    )
```
